512 devices in a mesh: gx: 8 (over z), gy: 8 (over y_hi, core), gz: 8 (over x, y_lo).
Axes of the slice: x: 4, y: 8 (y_hi: 4, y_lo: 2; y = y_hi * 2 + y_lo), z: 8, core: 2. Of those that a mesh axis runs over, the one named last changes fastest.
Arguments:
- density: float32 [32, 128, 1024], P('gx', 'gy', 'gz'), may hold values from 0.5 to 2
- momentum: float32 [3, 32, 128, 1024], P(None, 'gx', 'gy', 'gz'), may hold values from -1 to 1
- energy: float32 [32, 128, 1024], P('gx', 'gy', 'gz'), may hold values from 3 to 5
- cotangent: bfloat16 [5, 32, 128, 1024], P(None, 'gx', 'gy', 'gz'), may hold values from -6 to 6
- w_in: bfloat16 [64, 30], replicated, may hold values from -1 to 1
- b_in: float32 [64], replicated, may hold values from -3 to 3
- w_out: bfloat16 [5, 64], replicated, may hold values from -0.75 to 0.75
Outputs:
- residual: float32 [5, 32, 128, 1024], P(None, 'gx', 'gy', 'gz')
- state_adjoint: float32 [5, 32, 128, 1024], P(None, 'gx', 'gy', 'gz')
- grad_w_in: float32 [64, 30], replicated
- grad_b_in: float32 [64], replicated
- grad_w_out: float32 [5, 64], replicated
The draws below stay inside these ranges and needn't reach their ends.
All inputs are finite; a program needn't handle non-finite values.
Results may differ from the reference program's by a relative error of at most 0.025.
Values sent between devices are 32-bit elements; how exact they have to be, the bound alone decides.
A program may use at most 64 MiB of HBM per device.

```python
import jax
import jax.numpy as jnp
from jax import lax

HIDDEN_SIZE = 64
NX = 32
NY = 128
NZ = 1024


def levels(key, dims, shards, least, top_value):
    factor_of = 1.0
    for axis_at, parts in shards:
        steps = jax.random.uniform(jax.random.fold_in(jax.random.fold_in(key, 6), axis_at), (parts,), jnp.float32, least / len(shards), top_value / len(shards))
        factor_of = factor_of * jnp.repeat(jnp.exp(steps), dims[axis_at] // parts).reshape((-1,) + (1,) * (len(dims) - 1 - axis_at))
    return factor_of


def bell_draw(own_key, shape, spread, limit, cuts=(), dtype=jnp.bfloat16):
    drawn = spread * jax.random.normal(own_key, shape, jnp.float32)
    if cuts:
        drawn = drawn * levels(own_key, shape, cuts, -0.22, 0.18)
    return jnp.clip(drawn, -limit, limit).astype(dtype)


def setup_inputs(seed: int = 0) -> dict:
    streams_of = jax.random.split(jax.random.key(seed), 8)
    density = jnp.clip(0.5 + 1.5 * jax.random.uniform(streams_of[0], (NX, NY, NZ), jnp.float32) ** levels(streams_of[0], (NX, NY, NZ), ((0, 8), (1, 8), (2, 8)), -0.2, 0.2), 0.5, 2.0)
    momentum = jnp.clip(jax.random.uniform(streams_of[1], (3, NX, NY, NZ), jnp.float32, -1.0, 1.0) * levels(streams_of[1], (3, NX, NY, NZ), ((1, 8), (2, 8), (3, 8)), -0.4, 0.0), -1.0, 1.0)
    energy = jnp.clip(3.0 + 2.0 * jax.random.uniform(streams_of[2], (NX, NY, NZ), jnp.float32) ** levels(streams_of[2], (NX, NY, NZ), ((0, 8), (1, 8), (2, 8)), -0.2, 0.2), 3.0, 5.0)
    cotangent = bell_draw(streams_of[3], (5, NX, NY, NZ), 1.0, 6.0, ((1, 8), (2, 8), (3, 8)))
    w_in = bell_draw(streams_of[4], (HIDDEN_SIZE, 30), 30 ** -0.5, 1.0)
    b_in = bell_draw(streams_of[5], (HIDDEN_SIZE,), 0.5, 3.0, (), jnp.float32)
    w_out = bell_draw(streams_of[6], (5, HIDDEN_SIZE), HIDDEN_SIZE ** -0.5, 0.75)
    return {"density": density, "momentum": momentum, "energy": energy, "cotangent": cotangent, "w_in": w_in, "b_in": b_in, "w_out": w_out}


GAMMA_LESS = 0.4
ALPHA = 4.0
EPSILON = 1e-06

def euler_flux(cell, comp):
    density = cell[0]
    momentum = cell[1:4]
    energy = cell[4]
    speed = momentum[comp] / density
    pressure = GAMMA_LESS * (energy - 0.5 * lax.optimization_barrier(jnp.sum(momentum * momentum, axis=0)) / density)
    rows = [momentum[comp]]
    for index in range(3):
        term = momentum[index] * speed
        if index == comp:
            term = term + pressure
        rows.append(term)
    rows.append((energy + pressure) * speed)
    return jnp.stack(rows)

def weno_five(va, vb, vc, ve, vf):
    first = va - 2.0 * vb + vc
    second = vb - 2.0 * vc + ve
    third = vc - 2.0 * ve + vf
    beta_a = 13.0 / 12.0 * first * first + 0.25 * (va - 4.0 * vb + 3.0 * vc) * (va - 4.0 * vb + 3.0 * vc)
    beta_b = 13.0 / 12.0 * second * second + 0.25 * (vb - ve) * (vb - ve)
    beta_c = 13.0 / 12.0 * third * third + 0.25 * (3.0 * vc - 4.0 * ve + vf) * (3.0 * vc - 4.0 * ve + vf)
    alpha_a = 0.1 / ((EPSILON + beta_a) * (EPSILON + beta_a))
    alpha_b = 0.6 / ((EPSILON + beta_b) * (EPSILON + beta_b))
    alpha_c = 0.3 / ((EPSILON + beta_c) * (EPSILON + beta_c))
    cand_a = (2.0 * va - 7.0 * vb + 11.0 * vc) / 6.0
    cand_b = (-vb + 5.0 * vc + 2.0 * ve) / 6.0
    cand_c = (2.0 * vc + 5.0 * ve - vf) / 6.0
    return (alpha_a * cand_a + alpha_b * cand_b + alpha_c * cand_c) / (alpha_a + alpha_b + alpha_c)

def product(left, right):
    return jnp.dot(left.astype(jnp.float32), right.astype(jnp.float32), preferred_element_type=jnp.float32)

def local_pass(padded, lam, dim, w_in, b_in, w_out):
    count = padded.shape[dim] - 6
    faces = count + 1
    comp = dim - 1

    def front(pad):
        cells = [lax.slice_in_dim(pad, k, k + faces, axis=dim) for k in range(6)]
        fluxes = [euler_flux(c, comp) for c in cells]
        plus = [0.5 * (f + ALPHA * c) for f, c in zip(fluxes, cells)]
        minus = [0.5 * (f - ALPHA * c) for f, c in zip(fluxes, cells)]
        weno = weno_five(plus[0], plus[1], plus[2], plus[3], plus[4]) + weno_five(minus[5], minus[4], minus[3], minus[2], minus[1])
        return (weno, jnp.concatenate(cells, axis=0))
    (weno, feats), pull = jax.vjp(front, padded)
    feat_shape = feats.shape
    feats_low = feats.astype(jnp.bfloat16).reshape(feat_shape[0], -1)
    pre = product(w_in, feats_low) + b_in[:, None]
    act = jnp.tanh(pre)
    hidden = act.astype(jnp.bfloat16)
    corr = product(w_out, hidden).reshape(weno.shape)
    flux = weno + corr
    div_term = -(lax.slice_in_dim(flux, 1, faces, axis=dim) - lax.slice_in_dim(flux, 0, count, axis=dim))
    lam_wide = lam.astype(jnp.float32)
    zero_slab = jnp.zeros_like(lax.slice_in_dim(lam_wide, 0, 1, axis=dim))
    dflux = jnp.concatenate([lam_wide, zero_slab], axis=dim) - jnp.concatenate([zero_slab, lam_wide], axis=dim)
    dcorr = dflux.astype(jnp.bfloat16).reshape(5, -1)
    g_w_out = product(dcorr, hidden.T)
    dhid = product(w_out.T, dcorr)
    dpre = (dhid * (1.0 - act * act)).astype(jnp.bfloat16)
    g_w_in = product(dpre, feats_low.T)
    g_b_in = lax.optimization_barrier(jnp.sum(dpre.astype(jnp.float32), axis=1))
    dfeats = product(w_in.T, dpre).reshape(feat_shape)
    dpadded, = pull((dflux, dfeats))
    return (div_term, dpadded, g_w_in, g_b_in, g_w_out)

def spread_rims(from_left, from_right, count, dim):
    left_widths = [(0, 0)] * 4
    right_widths = [(0, 0)] * 4
    left_widths[dim] = (0, count - 3)
    right_widths[dim] = (count - 3, 0)
    return jnp.pad(from_left, left_widths) + jnp.pad(from_right, right_widths)

def sweep(padded, lam, dim, w_in, b_in, w_out):
    other = 2 if dim == 1 else 1
    width = 2 if padded.shape[other] % 2 == 0 else 1
    pieces = padded.shape[other] // width

    def split(arr):
        shape = arr.shape
        arr = arr.reshape(shape[:other] + (pieces, width) + shape[other + 1:])
        return jnp.moveaxis(arr, other, 0)

    def join(arr):
        arr = jnp.moveaxis(arr, 0, other)
        shape = arr.shape
        return arr.reshape(shape[:other] + (shape[other] * shape[other + 1],) + shape[other + 2:])

    def single(items):
        return local_pass(items[0], items[1], dim, w_in, b_in, w_out)
    div_term, dpadded, g_w_in, g_b_in, g_w_out = lax.map(single, (split(padded), split(lam)))
    return (join(div_term), join(dpadded), lax.optimization_barrier(jnp.sum(g_w_in, axis=0)), lax.optimization_barrier(jnp.sum(g_b_in, axis=0)), lax.optimization_barrier(jnp.sum(g_w_out, axis=0)))

def direction(state, lam, dim, w_in, b_in, w_out):
    size = state.shape[dim]
    padded = jnp.concatenate([lax.slice_in_dim(state, size - 3, size, axis=dim), state, lax.slice_in_dim(state, 0, 3, axis=dim)], axis=dim)
    div_term, dpadded, g_w_in, g_b_in, g_w_out = sweep(padded, lam, dim, w_in, b_in, w_out)
    total = dpadded.shape[dim]
    inner = lax.slice_in_dim(dpadded, 3, total - 3, axis=dim)
    from_left = lax.slice_in_dim(dpadded, total - 3, total, axis=dim)
    from_right = lax.slice_in_dim(dpadded, 0, 3, axis=dim)
    adjoint = inner + spread_rims(from_left, from_right, size, dim)
    return (div_term, adjoint, g_w_in, g_b_in, g_w_out)

def reference(density, momentum, energy, cotangent, w_in, b_in, w_out):
    state = jnp.concatenate([density[None], momentum, energy[None]], axis=0)
    residual = jnp.zeros_like(state)
    state_adjoint = jnp.zeros_like(state)
    grad_w_in = jnp.zeros(w_in.shape, jnp.float32)
    grad_b_in = jnp.zeros(b_in.shape, jnp.float32)
    grad_w_out = jnp.zeros(w_out.shape, jnp.float32)
    for dim in (1, 2, 3):
        div_term, adjoint, g_w_in, g_b_in, g_w_out = direction(state, cotangent, dim, w_in, b_in, w_out)
        residual = residual + div_term
        state_adjoint = state_adjoint + adjoint
        grad_w_in = grad_w_in + g_w_in
        grad_b_in = grad_b_in + g_b_in
        grad_w_out = grad_w_out + g_w_out
    return (residual, state_adjoint, grad_w_in, grad_b_in, grad_w_out)
```

```python
import functools

import jax
import jax.numpy as jnp
from jax import lax
from jax.experimental import pallas as pl
from jax.experimental.pallas import tpu as pltpu
from jax.sharding import PartitionSpec as P

F32 = jnp.float32
BF16 = jnp.bfloat16
AXES = ("gx", "gy", "gz")
MESH = pl.DeviceIdType.MESH
EPSILON = 1e-06
XC = 14
NT = (((1,), (1,)), ((), ()))


def recip(value):
    guess = pl.reciprocal(value, approx=True)
    return guess * (2.0 - value * guess)


def dot(left, right):
    return jnp.dot(left, right, preferred_element_type=F32)


def dot_nt(left, right):
    return lax.dot_general(left, right, NT, preferred_element_type=F32)


def line_weno(cells, cots):
    faces = len(cots)
    total = len(cells)
    diff = [cells[i + 1] - cells[i] for i in range(total - 1)]
    second = [None] + [diff[i] - diff[i - 1] for i in range(1, total - 1)]
    half = [None] + [0.5 * s for s in second[1:]]
    square = [None] + [EPSILON + (13.0 / 12.0) * s * s for s in second[1:]]
    third = [None] + [second[i + 1] - second[i] for i in range(1, total - 2)]
    values = []
    d_cell = [None] * total
    d_diff = [None] * total
    d_half = [None] * total
    d_square = [None] * total
    d_third = [None] * total

    def add(store, index, value):
        store[index] = value if store[index] is None else store[index] + value

    for k in range(faces):
        d1, d2 = diff[k + 1], diff[k + 2]
        t1, t2 = third[k + 1], third[k + 2]
        twice = t1 + t1
        pa = d1 + half[k + 1]
        pb = 0.5 * (d1 + d2)
        pc = d2 - half[k + 3]
        ra = recip(square[k + 1] + pa * pa)
        rb = recip(square[k + 2] + pb * pb)
        rc = recip(square[k + 3] + pc * pc)
        wa = ra * ra
        wb = 6.0 * (rb * rb)
        wc = 3.0 * (rc * rc)
        norm = recip(wa + wb + wc)
        y = (wa * twice + wc * t2) * norm
        values.append(cells[k + 2] + (1.0 / 6.0) * (d1 + (d2 + d2) - y))
        g = cots[k]
        sixth = (1.0 / 6.0) * g
        gn = sixth * norm
        ga = gn * wa
        gb = gn * wb
        gc = gn * wc
        ta = ga * ra * (twice - y)
        tb = gb * rb * y
        tc = gc * rc * (t2 - y)
        qa = 4.0 * (pa * ta)
        qb = 2.0 * (pb * tb)
        qc = 4.0 * (pc * tc)
        add(d_cell, k + 2, g)
        add(d_diff, k + 1, sixth + qa - qb)
        add(d_diff, k + 2, (sixth + sixth) + qc - qb)
        add(d_half, k + 1, qa)
        add(d_half, k + 3, -qc)
        add(d_square, k + 1, ta)
        add(d_square, k + 2, -tb)
        add(d_square, k + 3, tc)
        add(d_third, k + 1, -(ga + ga))
        add(d_third, k + 2, -gc)
    for i in range(1, total - 1):
        value = (13.0 / 3.0) * second[i] * d_square[i]
        if d_half[i] is not None:
            value = value + 0.5 * d_half[i]
        if d_third[i - 1] is not None:
            value = value + d_third[i - 1]
        if d_third[i] is not None:
            value = value - d_third[i]
        add(d_diff, i, value)
        add(d_diff, i - 1, -value)
    for i in range(total - 1):
        add(d_cell, i + 1, d_diff[i])
        add(d_cell, i, -d_diff[i])
    return values, d_cell


def kernel(
    sizes, dens, mom, ener, cot, w_in, b_in, w_out,
    res_o, adj_o, gwi_o, gbi_o, gwo_o,
    nat, lamn, vv, ll, fp, fm, dfp, dfm, dv, corr_s, res_s,
    zw, zl, w1, w1t, w2, w2t, hid, dpr, g1, g2, gm, ar, ar_in,
    ys, yr, zs, zr, xr, yb, ybr, zb, zbr, xbr,
    halo_send, halo_recv, back_send, back_recv, ar_send, ar_recv,
):
    me = [lax.axis_index(a) for a in AXES]

    def peer(axis, step):
        count = sizes[axis]
        return {AXES[axis]: lax.rem(me[axis] + (step % count), count)}

    bar = pltpu.get_barrier_semaphore()
    for axis in range(3):
        for step in range(1, sizes[axis]):
            pl.semaphore_signal(bar, 1, device_id=peer(axis, step), device_id_type=MESH)

    lane = lax.broadcasted_iota(jnp.int32, (64, 128), 1)
    low = lane < 64
    lane8 = lax.broadcasted_iota(jnp.int32, (3, 128), 1)
    low3 = lane8 < 64

    nat[0] = dens[...]
    nat[1:4] = mom[...]
    nat[4] = ener[...]
    lamn[...] = cot[...].astype(F32)

    def swap(value):
        return pltpu.roll(value, 64, 1)

    fields = [(nat, zw, 3, v) for v in range(5)] + [(lamn, zl, 0, v) for v in range(5)]
    for first, second in zip(fields[0::2], fields[1::2]):
        both = jnp.concatenate([first[0][first[3]], second[0][second[3]]], axis=0)
        turned = jnp.transpose(both)
        upper, lower = turned[0:64], turned[64:128]
        first[1][first[3], first[2] : first[2] + 64, :] = jnp.where(low, upper, swap(lower))
        second[1][second[3], second[2] : second[2] + 64, :] = jnp.where(low, swap(upper), lower)
    for v in range(5):
        zs[0, 3 * v : 3 * v + 3, :] = zw[v, 3:6, :]
        zs[1, 3 * v : 3 * v + 3, :] = zw[v, 64:67, :]
        for j in range(3):
            at = (3 * v + j) * 4
            ys[0, at : at + 4, :] = nat[v, pl.ds(j, 4, stride=16), :]
            ys[1, at : at + 4, :] = nat[v, pl.ds(13 + j, 4, stride=16), :]

    pl.semaphore_wait(bar, sum(sizes) - 3)

    def remote(src, dst, send, recv, index, axis, step):
        return pltpu.make_async_remote_copy(
            src_ref=src, dst_ref=dst, send_sem=send.at[index], recv_sem=recv.at[index],
            device_id=peer(axis, step), device_id_type=MESH,
        )

    halo = [
        remote(nat.at[:, 0:48, :], xr.at[1], halo_send, halo_recv, 0, 0, -1),
        remote(nat.at[:, 16:64, :], xr.at[0], halo_send, halo_recv, 1, 0, 1),
        remote(ys.at[0], yr.at[1], halo_send, halo_recv, 2, 1, -1),
        remote(ys.at[1], yr.at[0], halo_send, halo_recv, 3, 1, 1),
        remote(zs.at[0], zr.at[1], halo_send, halo_recv, 4, 2, -1),
        remote(zs.at[1], zr.at[0], halo_send, halo_recv, 5, 2, 1),
    ]
    for copy in halo:
        copy.start()

    def iota(shape, dim):
        return lax.broadcasted_iota(jnp.int32, shape, dim)

    def one_hot(shape, wide):
        return (iota(shape, wide) // 8 == iota(shape, 1 - wide)).astype(F32).astype(BF16)

    def same_row(shape):
        return (iota(shape, 0) % 8) == (iota(shape, 1) % 8)

    spread = one_hot((512, 64), 0)
    spread_t = one_hot((64, 512), 1)
    bias = b_in[...]
    bias_a = bias.astype(BF16).astype(F32)
    bias_b = (bias - bias_a).astype(BF16).astype(F32)
    bias_c = bias - bias_a - bias_b
    row = iota((256, 64), 0)
    bias_rows = jnp.where(row == 240, bias_a, jnp.where(row == 241, bias_b, jnp.where(row == 242, bias_c, 0.0)))
    wide_in = dot(w_in[...], one_hot((30, 256), 1)).astype(BF16)
    full_in = jnp.where(same_row((512, 256)), dot(spread, wide_in), 0.0)
    w1[...] = (full_in + dot_nt(spread, bias_rows.astype(BF16))).astype(BF16)
    tall_in = dot_nt(one_hot((240, 30), 0), w_in[...]).astype(BF16)
    w1t[...] = jnp.where(same_row((240, 512)), dot(tall_in, spread_t), 0.0).astype(BF16)
    tall_out = dot(one_hot((48, 5), 0), w_out[...]).astype(BF16)
    w2[...] = jnp.where(same_row((48, 512)), dot(tall_out, spread_t), 0.0).astype(BF16)
    wide_out = dot_nt(spread, w_out[...]).astype(BF16)
    w2t[...] = jnp.where(same_row((512, 48)), dot(wide_out, one_hot((5, 48), 1)), 0.0).astype(BF16)

    for v in range(5):
        for i in range(4):
            for t in range(2):
                at = i * 16 + t * 8
                vv[XC + 3 + i, 5 * t + v] = nat[v, at : at + 8, :]
                ll[11 + i, 5 * t + v] = lamn[v, at : at + 8, :]
        for r in range(14):
            for h in range(2):
                y = 8 * h + r - 3
                if 0 <= y < 16:
                    vv[r, v, 4 * h : 4 * h + 4, :] = nat[v, pl.ds(y, 4, stride=16), :]
        for j in range(8):
            vv[3 + j, 5 + v] = zw[v, pl.ds(3 + j, 8, stride=8), :]
            ll[1 + j, 5 + v] = zl[v, pl.ds(j, 8, stride=8), :]
            for h in range(2):
                ll[1 + j, v, 4 * h : 4 * h + 4, :] = lamn[v, pl.ds(8 * h + j, 4, stride=16), :]
    for end in (0, 9, 10, 15):
        ll[end] = jnp.zeros((10, 8, 128), F32)
    dv[...] = jnp.zeros(dv.shape, F32)
    g1[...] = jnp.zeros(g1.shape, F32)
    g2[...] = jnp.zeros(g2.shape, F32)

    for copy in halo[2:]:
        copy.wait_recv()
    for v in range(5):
        for j in range(3):
            at = (3 * v + j) * 4
            vv[j, v, 0:4, :] = yr[0, at : at + 4, :]
            vv[11 + j, v, 4:8, :] = yr[1, at : at + 4, :]
        zw[v, 0:3, :] = swap(jnp.where(low3, zw[v, 64:67, :], zr[0, 3 * v : 3 * v + 3, :]))
        zw[v, 67:70, :] = swap(jnp.where(low3, zr[1, 3 * v : 3 * v + 3, :], zw[v, 3:6, :]))
        for r in (0, 1, 2, 11, 12, 13):
            vv[r, 5 + v] = zw[v, pl.ds(r, 8, stride=8), :]

    ones = jnp.ones((16, 256), BF16)
    blank = jnp.zeros((8, 256), F32)

    def network(p, c0, lb):
        cells = [vv[pl.ds(c0, 6), 5 * t : 5 * t + 5].reshape(240, 128) for t in range(2)]
        feats = jnp.concatenate([jnp.concatenate(cells, axis=1).astype(BF16), ones], axis=0)
        steps = [(ll[lb + 1, 5 * t : 5 * t + 5] - ll[lb, 5 * t : 5 * t + 5]).reshape(40, 128) for t in range(2)]
        dcorr = jnp.concatenate([jnp.concatenate(steps, axis=1), blank], axis=0).astype(BF16)
        for part in range(4):
            rows = pl.ds(128 * part, 128)
            act = jnp.tanh(dot(w1[rows, :], feats))
            hid[rows, :] = act.astype(BF16)
            dpr[rows, :] = (dot(w2t[rows, :], dcorr) * (1.0 - act * act)).astype(BF16)
        corr = dot(w2[...], hid[...])
        dfeat = dot(w1t[...], dpr[...])
        for t in range(2):
            lanes = slice(128 * t, 128 * t + 128)
            corr_s[p, 5 * t : 5 * t + 5] = corr[0:40, lanes].reshape(5, 8, 128)
            dv[pl.ds(c0, 6), 5 * t : 5 * t + 5] += dfeat[:, lanes].reshape(6, 5, 8, 128)
        g1[...] += dot_nt(feats, dpr[...])
        g2[...] += dot_nt(dcorr, hid[...])

    def net_yz(p, carry):
        network(p, p, p)
        return carry

    lax.fori_loop(0, 9, net_yz, 0)

    for copy in halo[:2]:
        copy.wait_recv()
    for v in range(5):
        for i in range(3):
            for t in range(2):
                at = i * 16 + t * 8
                vv[XC + i, 5 * t + v] = xr[0, v, at : at + 8, :]
                vv[XC + 7 + i, 5 * t + v] = xr[1, v, at : at + 8, :]

    def net_x(k, carry):
        network(9 + k, XC + k, 10 + k)
        return carry

    lax.fori_loop(0, 5, net_x, 0)

    inner = jnp.where(same_row((240, 512)), g1[0:240, :], 0.0).reshape(30, 8, 512)
    outer = jnp.where(same_row((40, 512)), g2[0:40, :], 0.0).reshape(5, 8, 512)
    gm[0:30, :] = jnp.sum(inner, axis=1)
    gm[30:31, :] = g1[240:241, :]
    gm[31:36, :] = jnp.sum(outer, axis=1)
    gm[36:40, :] = jnp.zeros((4, 512), F32)
    gather = (iota((512, 128), 0) // 8 == iota((512, 128), 1)).astype(F32)
    packed = jnp.dot(gm[...], gather, preferred_element_type=F32, precision=lax.Precision.HIGHEST)
    ar[0, 0:16, :] = packed[0:16] + swap(packed[24:40])
    ar[0, 16:24, :] = packed[16:24]

    def reduce_copies(axis):
        return [
            pltpu.make_async_remote_copy(
                src_ref=ar.at[axis], dst_ref=ar_in.at[axis, me[axis]],
                send_sem=ar_send.at[axis, step], recv_sem=ar_recv.at[axis, step],
                device_id=peer(axis, step), device_id_type=MESH,
            )
            for step in range(1, sizes[axis])
        ]

    def reduce_start(axis):
        copies = reduce_copies(axis)
        for copy in copies:
            copy.start()
        ar_in[axis, me[axis]] = ar[axis]
        return copies

    def reduce_end(axis, copies):
        for copy in copies:
            copy.wait_recv()
        total = ar_in[axis, 0]
        for rank in range(1, sizes[axis]):
            total = total + ar_in[axis, rank]
        ar[axis + 1] = total

    def physics(cell, base, comp):
        u = [vv[cell, base + v] for v in range(5)]
        inverse = recip(u[0])
        speed = u[1 + comp] * inverse
        square = u[1] * u[1] + u[2] * u[2] + u[3] * u[3]
        pressure = 0.4 * (u[4] - 0.5 * square * inverse)
        return u, inverse, speed, square, pressure

    def split_flux(c0, count, base, comp):
        def step(c, carry):
            cell = c0 + c
            u, _, speed, _, pressure = physics(cell, base, comp)
            flux = [u[1 + comp]] + [u[1 + k] * speed for k in range(3)] + [(u[4] + pressure) * speed]
            flux[1 + comp] = flux[1 + comp] + pressure
            for v in range(5):
                part = 0.5 * flux[v]
                wave = 2.0 * u[v]
                fp[cell, base + v] = part + wave
                fm[cell, base + v] = part - wave
            return carry

        lax.fori_loop(0, count, step, 0)

    def pull_flux(c0, count, base, comp):
        def step(c, carry):
            cell = c0 + c
            u, inverse, speed, square, pressure = physics(cell, base, comp)
            plus = [dfp[cell, base + v] for v in range(5)]
            minus = [dfm[cell, base + v] for v in range(5)]
            df = [0.5 * (a + b) for a, b in zip(plus, minus)]
            du = [2.0 * (a - b) for a, b in zip(plus, minus)]
            d_speed = df[4] * (u[4] + pressure)
            for k in range(3):
                d_speed = d_speed + df[1 + k] * u[1 + k]
            d_energy = df[4] * speed
            d_press = 0.4 * (df[1 + comp] + d_energy)
            slope = d_press * inverse
            du[4] = du[4] + d_energy + d_press
            for k in range(3):
                du[1 + k] = du[1 + k] + df[1 + k] * speed - slope * u[1 + k]
            du[1 + comp] = du[1 + comp] + df[0] + d_speed * inverse
            d_inverse = d_speed * u[1 + comp] - 0.5 * square * d_press
            du[0] = du[0] - inverse * inverse * d_inverse
            for v in range(5):
                dv[cell, base + v] += du[v]
            return carry

        lax.fori_loop(0, count, step, 0)

    def weno(c0, l0, p0, r0, faces, first, last):
        def step(q, carry):
            plus = [fp[c0 + c, q] for c in range(faces + 4)]
            minus = [fm[c0 + c, q] for c in range(faces + 4, 0, -1)]
            lam = [ll[l0 + k, q] for k in range(faces + 1)]
            cots = [lam[k + 1] - lam[k] for k in range(faces)]
            value_p, d_plus = line_weno(plus, cots)
            value_m, d_minus = line_weno(minus, cots[::-1])
            flux = [value_p[k] + value_m[faces - 1 - k] + corr_s[p0 + k, q] for k in range(faces)]
            for c in range(faces - 1):
                res_s[r0 + c, q] = flux[c] - flux[c + 1]
            for c in range(faces + 4):
                dfp[c0 + c, q] = d_plus[c]
                dfm[c0 + faces + 4 - c, q] = d_minus[c]
            dfp[c0 + faces + 4, q] = jnp.zeros((8, 128), F32)
            dfm[c0, q] = jnp.zeros((8, 128), F32)
            return carry

        lax.fori_loop(first, last, step, 0)

    def back(src, dst, index, axis, step):
        return remote(src, dst, back_send, back_recv, index, axis, step)

    waiting = reduce_start(0)
    started = list(waiting)

    split_flux(XC, 10, 0, 0)
    split_flux(XC, 10, 5, 0)
    weno(XC, 10, 9, 8, 5, 0, 10)
    pull_flux(XC, 10, 0, 0)
    pull_flux(XC, 10, 5, 0)
    back_x = [back(dv.at[XC : XC + 3], xbr.at[1], 0, 0, -1), back(dv.at[XC + 7 : XC + 10], xbr.at[0], 1, 0, 1)]
    for copy in back_x:
        copy.start()

    reduce_end(0, waiting)
    waiting = reduce_start(1)
    started += waiting

    split_flux(0, 14, 5, 2)
    weno(0, 0, 0, 0, 9, 5, 10)
    pull_flux(0, 14, 5, 2)
    for v in range(5):
        for r in range(8):
            zw[v, pl.ds(r, 8, stride=8), :] = dv[r, 5 + v]
            zl[v, pl.ds(r, 8, stride=8), :] = res_s[r, 5 + v]
        zw[v, 64:72, :] = jnp.zeros((8, 128), F32)
        for r in range(8, 14):
            zw[v, pl.ds(r, 8, stride=8), :] += dv[r, 5 + v]
        zb[0, 3 * v : 3 * v + 3, :] = zw[v, 0:3, :]
        zb[1, 3 * v : 3 * v + 3, :] = zw[v, 67:70, :]
    back_z = [back(zb.at[0], zbr.at[1], 4, 2, -1), back(zb.at[1], zbr.at[0], 5, 2, 1)]
    for copy in back_z:
        copy.start()

    reduce_end(1, waiting)
    waiting = reduce_start(2)
    started += waiting

    split_flux(0, 14, 0, 1)
    weno(0, 0, 0, 0, 9, 0, 5)
    pull_flux(0, 14, 0, 1)
    for v in range(5):
        for j in range(3):
            at = (3 * v + j) * 4
            yb[0, at : at + 4, :] = dv[j, v, 0:4, :]
            yb[1, at : at + 4, :] = dv[11 + j, v, 4:8, :]
    back_y = [back(yb.at[0], ybr.at[1], 2, 1, -1), back(yb.at[1], ybr.at[0], 3, 1, 1)]
    for copy in back_y:
        copy.start()

    for copy in back_z:
        copy.wait_recv()
    for v in range(5):
        near = zw[v, 0:3, :]
        far = zw[v, 67:70, :]
        zw[v, 64:67, :] += swap(jnp.where(low3, zbr[1, 3 * v : 3 * v + 3, :], near))
        zw[v, 3:6, :] += swap(jnp.where(low3, far, zbr[0, 3 * v : 3 * v + 3, :]))
    fields = [(zw, adj_o, 3, v) for v in range(5)] + [(zl, res_o, 0, v) for v in range(5)]
    for first, second in zip(fields[0::2], fields[1::2]):
        one = first[0][first[3], first[2] : first[2] + 64, :]
        two = second[0][second[3], second[2] : second[2] + 64, :]
        upper = jnp.where(low, one, swap(two))
        lower = jnp.where(low, swap(one), two)
        turned = jnp.transpose(jnp.concatenate([upper, lower], axis=0))
        first[1][first[3]] = turned[0:64]
        second[1][second[3]] = turned[64:128]

    for copy in back_x:
        copy.wait_recv()
    for v in range(5):
        for i in range(4):
            for t in range(2):
                at = i * 16 + t * 8
                value = dv[XC + 3 + i, 5 * t + v]
                if i < 3:
                    value = value + xbr[0, i, 5 * t + v]
                if i > 0:
                    value = value + xbr[1, i - 1, 5 * t + v]
                adj_o[v, at : at + 8, :] += value
                res_o[v, at : at + 8, :] += res_s[8 + i, 5 * t + v]

    for v in range(5):
        for r in range(14):
            for h in range(2):
                y = 8 * h + r - 3
                if 0 <= y < 16:
                    adj_o[v, pl.ds(y, 4, stride=16), :] += dv[r, v, 4 * h : 4 * h + 4, :]
        for j in range(8):
            for h in range(2):
                res_o[v, pl.ds(8 * h + j, 4, stride=16), :] += res_s[j, v, 4 * h : 4 * h + 4, :]
    for copy in back_y:
        copy.wait_recv()
    for v in range(5):
        for j in range(3):
            at = (3 * v + j) * 4
            adj_o[v, pl.ds(j, 4, stride=16), :] += ybr[0, at : at + 4, :]
            adj_o[v, pl.ds(13 + j, 4, stride=16), :] += ybr[1, at : at + 4, :]

    reduce_end(2, waiting)
    gwi_o[...] = jnp.transpose(jnp.concatenate([ar[3], swap(ar[3, 0:8, :])], axis=0))[0:64, 0:30]
    gm[0:16, 0:128] = swap(ar[3, 0:16, :])
    gbi_o[...] = gm[6:7, 0:64]
    gwo_o[...] = gm[7:12, 0:64]

    for copy in halo + started + back_x + back_y + back_z:
        copy.wait_send()


def per_device(density, momentum, energy, cotangent, w_in, b_in, w_out):
    sizes = tuple(lax.axis_size(a) for a in AXES)
    most = max(sizes)
    vmem = pl.BlockSpec(memory_space=pltpu.VMEM)
    tiles = lambda n: pltpu.VMEM((n, 10, 8, 128), F32)
    dma = pltpu.SemaphoreType.DMA
    out = pl.pallas_call(
        functools.partial(kernel, sizes),
        out_shape=(
            jax.ShapeDtypeStruct((5, 64, 128), F32),
            jax.ShapeDtypeStruct((5, 64, 128), F32),
            jax.ShapeDtypeStruct((64, 30), F32),
            jax.ShapeDtypeStruct((1, 64), F32),
            jax.ShapeDtypeStruct((5, 64), F32),
        ),
        in_specs=[vmem] * 7,
        out_specs=(vmem,) * 5,
        scratch_shapes=[
            pltpu.VMEM((5, 64, 128), F32), pltpu.VMEM((5, 64, 128), F32),
            tiles(24), tiles(16), tiles(24), tiles(24), tiles(24), tiles(24), tiles(24), tiles(14), tiles(12),
            pltpu.VMEM((5, 72, 128), F32), pltpu.VMEM((5, 64, 128), F32),
            pltpu.VMEM((512, 256), BF16), pltpu.VMEM((240, 512), BF16),
            pltpu.VMEM((48, 512), BF16), pltpu.VMEM((512, 48), BF16),
            pltpu.VMEM((512, 256), BF16), pltpu.VMEM((512, 256), BF16),
            pltpu.VMEM((256, 512), F32), pltpu.VMEM((48, 512), F32), pltpu.VMEM((40, 512), F32),
            pltpu.VMEM((4, 24, 128), F32), pltpu.VMEM((3, most, 24, 128), F32),
            pltpu.VMEM((2, 64, 128), F32), pltpu.VMEM((2, 64, 128), F32),
            pltpu.VMEM((2, 16, 128), F32), pltpu.VMEM((2, 16, 128), F32),
            pltpu.VMEM((2, 5, 48, 128), F32),
            pltpu.VMEM((2, 64, 128), F32), pltpu.VMEM((2, 64, 128), F32),
            pltpu.VMEM((2, 16, 128), F32), pltpu.VMEM((2, 16, 128), F32),
            pltpu.VMEM((2, 3, 10, 8, 128), F32),
            dma((6,)), dma((6,)), dma((6,)), dma((6,)), dma((3, most)), dma((3, most)),
        ],
        compiler_params=pltpu.CompilerParams(
            collective_id=0, has_side_effects=True, vmem_limit_bytes=40 * 1024 * 1024
        ),
        name="section",
    )(
        density.reshape(64, 128), momentum.reshape(3, 64, 128), energy.reshape(64, 128),
        cotangent.reshape(5, 64, 128), w_in, b_in[None, :], w_out,
    )
    residual, adjoint, grad_w_in, grad_b_in, grad_w_out = out
    return (
        residual.reshape(5, 4, 16, 128), adjoint.reshape(5, 4, 16, 128),
        grad_w_in, grad_b_in[0], grad_w_out,
    )


def solution(mesh):
    return jax.shard_map(
        per_device,
        mesh=mesh,
        in_specs=(
            P("gx", "gy", "gz"),
            P(None, "gx", "gy", "gz"),
            P("gx", "gy", "gz"),
            P(None, "gx", "gy", "gz"),
            P(),
            P(),
            P(),
        ),
        out_specs=(P(None, "gx", "gy", "gz"), P(None, "gx", "gy", "gz"), P(), P(), P()),
        check_vma=False,
    )
```

```python
import functools

import jax
import jax.numpy as jnp
from jax import lax
from jax.experimental import pallas as pl
from jax.experimental.pallas import tpu as pltpu
from jax.sharding import PartitionSpec as P

F32 = jnp.float32
BF16 = jnp.bfloat16
AXES = ("gx", "gy", "gz")
MESH = pl.DeviceIdType.MESH
EPSILON = 1e-06
XC = 14
NT = (((1,), (1,)), ((), ()))


def recip(value):
    guess = pl.reciprocal(value, approx=True)
    return guess * (2.0 - value * guess)


def dot(left, right):
    return jnp.dot(left, right, preferred_element_type=F32)


def dot_nt(left, right):
    return lax.dot_general(left, right, NT, preferred_element_type=F32)


def line_weno(cells, cots):
    faces = len(cots)
    total = len(cells)
    diff = [cells[i + 1] - cells[i] for i in range(total - 1)]
    second = [None] + [diff[i] - diff[i - 1] for i in range(1, total - 1)]
    half = [None] + [0.5 * s for s in second[1:]]
    square = [None] + [EPSILON + (13.0 / 12.0) * s * s for s in second[1:]]
    third = [None] + [second[i + 1] - second[i] for i in range(1, total - 2)]
    values = []
    d_cell = [None] * total
    d_diff = [None] * total
    d_half = [None] * total
    d_square = [None] * total
    d_third = [None] * total

    def add(store, index, value):
        store[index] = value if store[index] is None else store[index] + value

    for k in range(faces):
        d1, d2 = diff[k + 1], diff[k + 2]
        t1, t2 = third[k + 1], third[k + 2]
        twice = t1 + t1
        pa = d1 + half[k + 1]
        pb = 0.5 * (d1 + d2)
        pc = d2 - half[k + 3]
        ra = recip(square[k + 1] + pa * pa)
        rb = recip(square[k + 2] + pb * pb)
        rc = recip(square[k + 3] + pc * pc)
        wa = ra * ra
        wb = 6.0 * (rb * rb)
        wc = 3.0 * (rc * rc)
        norm = recip(wa + wb + wc)
        y = (wa * twice + wc * t2) * norm
        values.append(cells[k + 2] + (1.0 / 6.0) * (d1 + (d2 + d2) - y))
        g = cots[k]
        sixth = (1.0 / 6.0) * g
        gn = sixth * norm
        ga = gn * wa
        gb = gn * wb
        gc = gn * wc
        ta = ga * ra * (twice - y)
        tb = gb * rb * y
        tc = gc * rc * (t2 - y)
        qa = 4.0 * (pa * ta)
        qb = 2.0 * (pb * tb)
        qc = 4.0 * (pc * tc)
        add(d_cell, k + 2, g)
        add(d_diff, k + 1, sixth + qa - qb)
        add(d_diff, k + 2, (sixth + sixth) + qc - qb)
        add(d_half, k + 1, qa)
        add(d_half, k + 3, -qc)
        add(d_square, k + 1, ta)
        add(d_square, k + 2, -tb)
        add(d_square, k + 3, tc)
        add(d_third, k + 1, -(ga + ga))
        add(d_third, k + 2, -gc)
    for i in range(1, total - 1):
        value = (13.0 / 3.0) * second[i] * d_square[i]
        if d_half[i] is not None:
            value = value + 0.5 * d_half[i]
        if d_third[i - 1] is not None:
            value = value + d_third[i - 1]
        if d_third[i] is not None:
            value = value - d_third[i]
        add(d_diff, i, value)
        add(d_diff, i - 1, -value)
    for i in range(total - 1):
        add(d_cell, i + 1, d_diff[i])
        add(d_cell, i, -d_diff[i])
    return values, d_cell


def kernel(
    sizes, dens, mom, ener, cot, w_in_h, b_in_h, w_out_h,
    res_o, adj_o, grad_o,
    cotv, w_in, b_in, w_out, fea, dco, nat, lamn, vv, ll, fp, fm, dfp, dfm, dv, corr_s, res_s,
    zw, zl, w1, w1t, w2, w2t, hid, dpr, g1, g2, gm, ar, ar_in,
    ys, yr, zs, zr, xr, yb, ybr, zb, zbr, xbr,
    halo_send, halo_recv, back_send, back_recv, ar_send, ar_recv, load_sem,
):
    me = [lax.axis_index(a) for a in AXES]

    def peer(axis, step):
        count = sizes[axis]
        return {AXES[axis]: lax.rem(me[axis] + (step % count), count)}

    bar = pltpu.get_barrier_semaphore()
    for axis in range(3):
        for step in range(1, sizes[axis]):
            pl.semaphore_signal(bar, 1, device_id=peer(axis, step), device_id_type=MESH)

    loads = [
        pltpu.make_async_copy(src, dst, load_sem.at[index])
        for index, (src, dst) in enumerate((
            (dens, nat.at[0]), (mom, nat.at[1:4]), (ener, nat.at[4]), (cot, cotv),
            (w_in_h, w_in), (b_in_h, b_in), (w_out_h, w_out),
        ))
    ]
    for copy in loads:
        copy.start()

    lane = lax.broadcasted_iota(jnp.int32, (64, 128), 1)
    low = lane < 64
    lane8 = lax.broadcasted_iota(jnp.int32, (3, 128), 1)
    low3 = lane8 < 64

    for copy in loads:
        copy.wait()
    lamn[...] = cotv[...].astype(F32)

    def swap(value):
        return pltpu.roll(value, 64, 1)

    fields = [(nat, zw, 3, v) for v in range(5)] + [(lamn, zl, 0, v) for v in range(5)]
    for first, second in zip(fields[0::2], fields[1::2]):
        both = jnp.concatenate([first[0][first[3]], second[0][second[3]]], axis=0)
        turned = jnp.transpose(both)
        upper, lower = turned[0:64], turned[64:128]
        first[1][first[3], first[2] : first[2] + 64, :] = jnp.where(low, upper, swap(lower))
        second[1][second[3], second[2] : second[2] + 64, :] = jnp.where(low, swap(upper), lower)
    for v in range(5):
        zs[0, 3 * v : 3 * v + 3, :] = zw[v, 3:6, :]
        zs[1, 3 * v : 3 * v + 3, :] = zw[v, 64:67, :]
        for j in range(3):
            at = (3 * v + j) * 4
            ys[0, at : at + 4, :] = nat[v, pl.ds(j, 4, stride=16), :]
            ys[1, at : at + 4, :] = nat[v, pl.ds(13 + j, 4, stride=16), :]

    pl.semaphore_wait(bar, sum(sizes) - 3)

    def remote(src, dst, send, recv, index, axis, step):
        return pltpu.make_async_remote_copy(
            src_ref=src, dst_ref=dst, send_sem=send.at[index], recv_sem=recv.at[index],
            device_id=peer(axis, step), device_id_type=MESH,
        )

    halo = [
        remote(nat.at[:, 0:48, :], xr.at[1], halo_send, halo_recv, 0, 0, -1),
        remote(nat.at[:, 16:64, :], xr.at[0], halo_send, halo_recv, 1, 0, 1),
        remote(ys.at[0], yr.at[1], halo_send, halo_recv, 2, 1, -1),
        remote(ys.at[1], yr.at[0], halo_send, halo_recv, 3, 1, 1),
        remote(zs.at[0], zr.at[1], halo_send, halo_recv, 4, 2, -1),
        remote(zs.at[1], zr.at[0], halo_send, halo_recv, 5, 2, 1),
    ]
    for copy in halo:
        copy.start()

    def iota(shape, dim):
        return lax.broadcasted_iota(jnp.int32, shape, dim)

    def one_hot(shape, wide):
        return (iota(shape, wide) // 8 == iota(shape, 1 - wide)).astype(F32).astype(BF16)

    def same_row(shape):
        return (iota(shape, 0) % 8) == (iota(shape, 1) % 8)

    spread = one_hot((512, 64), 0)
    spread_t = one_hot((64, 512), 1)
    bias = b_in[...]
    bias_a = bias.astype(BF16).astype(F32)
    bias_b = (bias - bias_a).astype(BF16).astype(F32)
    bias_c = bias - bias_a - bias_b
    row = iota((256, 64), 0)
    bias_rows = jnp.where(row == 240, bias_a, jnp.where(row == 241, bias_b, jnp.where(row == 242, bias_c, 0.0)))
    tall_in = (dot(one_hot((256, 30), 0), w_in[...]) + bias_rows).astype(BF16)
    kept = same_row((512, 256)) | (iota((512, 256), 1) >= 240)
    w1[...] = jnp.where(kept, dot_nt(spread, tall_in), 0.0).astype(BF16)
    w1t[...] = jnp.where(same_row((240, 512)), dot(tall_in[0:240], spread_t), 0.0).astype(BF16)
    tall_out = dot(one_hot((48, 5), 0), w_out[...]).astype(BF16)
    w2[...] = jnp.where(same_row((48, 512)), dot(tall_out, spread_t), 0.0).astype(BF16)
    wide_out = dot_nt(spread, w_out[...]).astype(BF16)
    w2t[...] = jnp.where(same_row((512, 48)), dot(wide_out, one_hot((5, 48), 1)), 0.0).astype(BF16)

    for v in range(5):
        for i in range(4):
            for t in range(2):
                at = i * 16 + t * 8
                vv[XC + 3 + i, 5 * t + v] = nat[v, at : at + 8, :]
                ll[11 + i, 5 * t + v] = lamn[v, at : at + 8, :]
        for r in range(14):
            for h in range(2):
                y = 8 * h + r - 3
                if 0 <= y < 16:
                    vv[r, v, 4 * h : 4 * h + 4, :] = nat[v, pl.ds(y, 4, stride=16), :]
        for j in range(8):
            vv[3 + j, 5 + v] = zw[v, pl.ds(3 + j, 8, stride=8), :]
            ll[1 + j, 5 + v] = zl[v, pl.ds(j, 8, stride=8), :]
            for h in range(2):
                ll[1 + j, v, 4 * h : 4 * h + 4, :] = lamn[v, pl.ds(8 * h + j, 4, stride=16), :]
    for end in (0, 9, 10, 15):
        ll[end] = jnp.zeros((10, 8, 128), F32)
    dv[...] = jnp.zeros(dv.shape, F32)
    g1[...] = jnp.zeros(g1.shape, F32)
    g2[...] = jnp.zeros(g2.shape, F32)

    ones = jnp.ones((16, 256), BF16)
    blank = jnp.zeros((8, 256), F32)

    def network(p0, c0, l0, count):
        for f in range(count):
            cells = [vv[pl.ds(c0 + f, 6), 5 * t : 5 * t + 5].reshape(240, 128) for t in range(2)]
            feats = jnp.concatenate([jnp.concatenate(cells, axis=1).astype(BF16), ones], axis=0)
            steps = [
                (ll[l0 + f + 1, 5 * t : 5 * t + 5] - ll[l0 + f, 5 * t : 5 * t + 5]).reshape(40, 128) for t in range(2)
            ]
            dcorr = jnp.concatenate([jnp.concatenate(steps, axis=1), blank], axis=0).astype(BF16)
            lanes = slice(256 * f, 256 * f + 256)
            fea[:, lanes] = feats
            dco[:, lanes] = dcorr
            for part in range(4):
                rows = slice(128 * part, 128 * part + 128)
                act = jnp.tanh(dot(w1[rows, :], feats))
                hid[rows, lanes] = act.astype(BF16)
                dpr[rows, lanes] = (dot(w2t[rows, :], dcorr) * (1.0 - act * act)).astype(BF16)
        wide = slice(0, 256 * count)
        total = {}
        for f in range(count):
            lanes = slice(256 * f, 256 * f + 256)
            corr = dot(w2[...], hid[:, lanes])
            dfeat = dot(w1t[...], dpr[:, lanes])
            for t in range(2):
                tile = slice(128 * t, 128 * t + 128)
                corr_s[p0 + f, 5 * t : 5 * t + 5] = corr[0:40, tile].reshape(5, 8, 128)
                for c in range(6):
                    part = dfeat[40 * c : 40 * c + 40, tile].reshape(5, 8, 128)
                    total[f + c, t] = part if (f + c, t) not in total else total[f + c, t] + part
        for (c, t), part in total.items():
            dv[c0 + c, 5 * t : 5 * t + 5] += part
        g1[...] += dot_nt(fea[:, wide], dpr[:, wide])
        g2[...] += dot_nt(dco[:, wide], hid[:, wide])

    network(3, 3, 3, 3)

    for copy in halo[2:]:
        copy.wait_recv()
    for v in range(5):
        for j in range(3):
            at = (3 * v + j) * 4
            vv[j, v, 0:4, :] = yr[0, at : at + 4, :]
            vv[11 + j, v, 4:8, :] = yr[1, at : at + 4, :]
        zw[v, 0:3, :] = swap(jnp.where(low3, zw[v, 64:67, :], zr[0, 3 * v : 3 * v + 3, :]))
        zw[v, 67:70, :] = swap(jnp.where(low3, zr[1, 3 * v : 3 * v + 3, :], zw[v, 3:6, :]))
        for r in (0, 1, 2, 11, 12, 13):
            vv[r, 5 + v] = zw[v, pl.ds(r, 8, stride=8), :]

    def net_yz(i, carry):
        network(6 * i, 6 * i, 6 * i, 3)
        return carry

    lax.fori_loop(0, 2, net_yz, 0)

    for copy in halo[:2]:
        copy.wait_recv()
    for v in range(5):
        for i in range(3):
            for t in range(2):
                at = i * 16 + t * 8
                vv[XC + i, 5 * t + v] = xr[0, v, at : at + 8, :]
                vv[XC + 7 + i, 5 * t + v] = xr[1, v, at : at + 8, :]
    network(9, XC, 10, 5)

    inner = jnp.where(same_row((240, 512)), g1[0:240, :], 0.0).reshape(30, 8, 512)
    outer = jnp.where(same_row((40, 512)), g2[0:40, :], 0.0).reshape(5, 8, 512)
    gm[0:30, :] = jnp.sum(inner, axis=1)
    gm[30:31, :] = g1[240:241, :]
    gm[31:36, :] = jnp.sum(outer, axis=1)
    gm[36:40, :] = jnp.zeros((4, 512), F32)
    gather = (iota((512, 128), 0) // 8 == iota((512, 128), 1)).astype(F32)
    packed = jnp.dot(gm[...], gather, preferred_element_type=F32, precision=lax.Precision.HIGHEST)
    ar[0, 0:16, :] = packed[0:16] + swap(packed[24:40])
    ar[0, 16:24, :] = packed[16:24]

    order = (2, 1, 0)

    def reduce_start(phase):
        axis = order[phase]
        copies = [
            pltpu.make_async_remote_copy(
                src_ref=ar.at[phase], dst_ref=ar_in.at[phase, me[axis]],
                send_sem=ar_send.at[phase, step], recv_sem=ar_recv.at[phase, step],
                device_id=peer(axis, step), device_id_type=MESH,
            )
            for step in range(1, sizes[axis])
        ]
        for copy in copies:
            copy.start()
        ar_in[phase, me[axis]] = ar[phase]
        return copies

    def reduce_end(phase, copies):
        for copy in copies:
            copy.wait_recv()
        total = ar_in[phase, 0]
        for rank in range(1, sizes[order[phase]]):
            total = total + ar_in[phase, rank]
        ar[phase + 1] = total

    def physics(cell, base, comp):
        u = [vv[cell, base + v] for v in range(5)]
        inverse = recip(u[0])
        speed = u[1 + comp] * inverse
        square = u[1] * u[1] + u[2] * u[2] + u[3] * u[3]
        pressure = 0.4 * (u[4] - 0.5 * square * inverse)
        return u, inverse, speed, square, pressure

    def split_flux(c0, count, base, comp):
        def step(c, carry):
            cell = c0 + c
            u, _, speed, _, pressure = physics(cell, base, comp)
            flux = [u[1 + comp]] + [u[1 + k] * speed for k in range(3)] + [(u[4] + pressure) * speed]
            flux[1 + comp] = flux[1 + comp] + pressure
            for v in range(5):
                part = 0.5 * flux[v]
                wave = 2.0 * u[v]
                fp[cell, base + v] = part + wave
                fm[cell, base + v] = part - wave
            return carry

        lax.fori_loop(0, count, step, 0, unroll=count // 2)

    def pull_flux(c0, count, base, comp):
        def step(c, carry):
            cell = c0 + c
            u, inverse, speed, square, pressure = physics(cell, base, comp)
            plus = [dfp[cell, base + v] for v in range(5)]
            minus = [dfm[cell, base + v] for v in range(5)]
            df = [0.5 * (a + b) for a, b in zip(plus, minus)]
            du = [2.0 * (a - b) for a, b in zip(plus, minus)]
            d_speed = df[4] * (u[4] + pressure)
            for k in range(3):
                d_speed = d_speed + df[1 + k] * u[1 + k]
            d_energy = df[4] * speed
            d_press = 0.4 * (df[1 + comp] + d_energy)
            slope = d_press * inverse
            du[4] = du[4] + d_energy + d_press
            for k in range(3):
                du[1 + k] = du[1 + k] + df[1 + k] * speed - slope * u[1 + k]
            du[1 + comp] = du[1 + comp] + df[0] + d_speed * inverse
            d_inverse = d_speed * u[1 + comp] - 0.5 * square * d_press
            du[0] = du[0] - inverse * inverse * d_inverse
            for v in range(5):
                dv[cell, base + v] += du[v]
            return carry

        lax.fori_loop(0, count, step, 0, unroll=count // 2)

    def weno(c0, l0, p0, r0, faces, first, last):
        def step(q, carry):
            plus = [fp[c0 + c, q] for c in range(faces + 4)]
            minus = [fm[c0 + c, q] for c in range(faces + 4, 0, -1)]
            lam = [ll[l0 + k, q] for k in range(faces + 1)]
            cots = [lam[k + 1] - lam[k] for k in range(faces)]
            value_p, d_plus = line_weno(plus, cots)
            value_m, d_minus = line_weno(minus, cots[::-1])
            flux = [value_p[k] + value_m[faces - 1 - k] + corr_s[p0 + k, q] for k in range(faces)]
            for c in range(faces - 1):
                res_s[r0 + c, q] = flux[c] - flux[c + 1]
            for c in range(faces + 4):
                dfp[c0 + c, q] = d_plus[c]
                dfm[c0 + faces + 4 - c, q] = d_minus[c]
            dfp[c0 + faces + 4, q] = jnp.zeros((8, 128), F32)
            dfm[c0, q] = jnp.zeros((8, 128), F32)
            return carry

        lax.fori_loop(first, last, step, 0)

    def back(src, dst, index, axis, step):
        return remote(src, dst, back_send, back_recv, index, axis, step)

    waiting = reduce_start(0)
    started = list(waiting)

    split_flux(XC, 10, 0, 0)
    split_flux(XC, 10, 5, 0)
    weno(XC, 10, 9, 8, 5, 0, 10)
    pull_flux(XC, 10, 0, 0)
    pull_flux(XC, 10, 5, 0)
    back_x = [back(dv.at[XC : XC + 3], xbr.at[1], 0, 0, -1), back(dv.at[XC + 7 : XC + 10], xbr.at[0], 1, 0, 1)]
    for copy in back_x:
        copy.start()

    reduce_end(0, waiting)
    waiting = reduce_start(1)
    started += waiting

    split_flux(0, 14, 5, 2)
    weno(0, 0, 0, 0, 9, 5, 10)
    pull_flux(0, 14, 5, 2)
    for v in range(5):
        for r in range(8):
            zw[v, pl.ds(r, 8, stride=8), :] = dv[r, 5 + v]
            zl[v, pl.ds(r, 8, stride=8), :] = res_s[r, 5 + v]
        zw[v, 64:72, :] = jnp.zeros((8, 128), F32)
        for r in range(8, 14):
            zw[v, pl.ds(r, 8, stride=8), :] += dv[r, 5 + v]
        zb[0, 3 * v : 3 * v + 3, :] = zw[v, 0:3, :]
        zb[1, 3 * v : 3 * v + 3, :] = zw[v, 67:70, :]
    back_z = [back(zb.at[0], zbr.at[1], 4, 2, -1), back(zb.at[1], zbr.at[0], 5, 2, 1)]
    for copy in back_z:
        copy.start()

    reduce_end(1, waiting)
    waiting = reduce_start(2)
    started += waiting

    split_flux(0, 14, 0, 1)
    weno(0, 0, 0, 0, 9, 0, 5)
    pull_flux(0, 14, 0, 1)
    for v in range(5):
        for j in range(3):
            at = (3 * v + j) * 4
            yb[0, at : at + 4, :] = dv[j, v, 0:4, :]
            yb[1, at : at + 4, :] = dv[11 + j, v, 4:8, :]
    back_y = [back(yb.at[0], ybr.at[1], 2, 1, -1), back(yb.at[1], ybr.at[0], 3, 1, 1)]
    for copy in back_y:
        copy.start()

    for copy in back_z:
        copy.wait_recv()
    for v in range(5):
        near = zw[v, 0:3, :]
        far = zw[v, 67:70, :]
        zw[v, 64:67, :] += swap(jnp.where(low3, zbr[1, 3 * v : 3 * v + 3, :], near))
        zw[v, 3:6, :] += swap(jnp.where(low3, far, zbr[0, 3 * v : 3 * v + 3, :]))
    fields = [(zw, adj_o, 3, v) for v in range(5)] + [(zl, res_o, 0, v) for v in range(5)]
    for first, second in zip(fields[0::2], fields[1::2]):
        one = first[0][first[3], first[2] : first[2] + 64, :]
        two = second[0][second[3], second[2] : second[2] + 64, :]
        upper = jnp.where(low, one, swap(two))
        lower = jnp.where(low, swap(one), two)
        turned = jnp.transpose(jnp.concatenate([upper, lower], axis=0))
        first[1][first[3]] = turned[0:64]
        second[1][second[3]] = turned[64:128]

    for copy in back_x:
        copy.wait_recv()
    for v in range(5):
        for i in range(4):
            for t in range(2):
                at = i * 16 + t * 8
                value = dv[XC + 3 + i, 5 * t + v]
                if i < 3:
                    value = value + xbr[0, i, 5 * t + v]
                if i > 0:
                    value = value + xbr[1, i - 1, 5 * t + v]
                adj_o[v, at : at + 8, :] += value
                res_o[v, at : at + 8, :] += res_s[8 + i, 5 * t + v]

    for v in range(5):
        for r in range(14):
            for h in range(2):
                y = 8 * h + r - 3
                if 0 <= y < 16:
                    adj_o[v, pl.ds(y, 4, stride=16), :] += dv[r, v, 4 * h : 4 * h + 4, :]
        for j in range(8):
            for h in range(2):
                res_o[v, pl.ds(8 * h + j, 4, stride=16), :] += res_s[j, v, 4 * h : 4 * h + 4, :]
    for copy in back_y:
        copy.wait_recv()
    for v in range(5):
        for j in range(3):
            at = (3 * v + j) * 4
            adj_o[v, pl.ds(j, 4, stride=16), :] += ybr[0, at : at + 4, :]
            adj_o[v, pl.ds(13 + j, 4, stride=16), :] += ybr[1, at : at + 4, :]

    reduce_end(2, waiting)
    grad_o[0:24, :] = ar[3]
    grad_o[24:40, :] = swap(ar[3, 0:16, :])

    for copy in halo + started + back_x + back_y + back_z:
        copy.wait_send()


def finish(res, adj, grad, res_h, adj_h, gwi_h, gbi_h, gwo_h, gwi, gbi, gwo, sems):
    gwi[...] = grad[0:30, 0:64]
    gbi[...] = grad[30:31, 0:64]
    gwo[...] = grad[31:36, 0:64]
    pairs = ((res, res_h), (adj, adj_h), (gwi, gwi_h), (gbi, gbi_h), (gwo, gwo_h))
    copies = [pltpu.make_async_copy(src, dst, sems.at[index]) for index, (src, dst) in enumerate(pairs)]
    for copy in copies:
        copy.start()
    for copy in copies:
        copy.wait()


def per_device(density, momentum, energy, cotangent, w_in, b_in, w_out):
    sizes = tuple(lax.axis_size(a) for a in AXES)
    most = max(sizes)
    vmem = pl.BlockSpec(memory_space=pltpu.VMEM)
    hbm = pl.BlockSpec(memory_space=pltpu.HBM)
    tiles = lambda n: pltpu.VMEM((n, 10, 8, 128), F32)
    dma = pltpu.SemaphoreType.DMA
    block = jax.ShapeDtypeStruct((5, 64, 128), F32)
    residual, adjoint, grads = pl.pallas_call(
        functools.partial(kernel, sizes),
        out_shape=(block, block, jax.ShapeDtypeStruct((40, 128), F32)),
        in_specs=[hbm] * 7,
        out_specs=(vmem,) * 3,
        scratch_shapes=[
            pltpu.VMEM((5, 64, 128), BF16), pltpu.VMEM((30, 64), BF16),
            pltpu.VMEM((1, 64), F32), pltpu.VMEM((5, 64), BF16),
            pltpu.VMEM((256, 1280), BF16), pltpu.VMEM((48, 1280), BF16),
            pltpu.VMEM((5, 64, 128), F32), pltpu.VMEM((5, 64, 128), F32),
            tiles(24), tiles(16), tiles(24), tiles(24), tiles(24), tiles(24), tiles(24), tiles(14), tiles(12),
            pltpu.VMEM((5, 72, 128), F32), pltpu.VMEM((5, 64, 128), F32),
            pltpu.VMEM((512, 256), BF16), pltpu.VMEM((240, 512), BF16),
            pltpu.VMEM((48, 512), BF16), pltpu.VMEM((512, 48), BF16),
            pltpu.VMEM((512, 1280), BF16), pltpu.VMEM((512, 1280), BF16),
            pltpu.VMEM((256, 512), F32), pltpu.VMEM((48, 512), F32), pltpu.VMEM((40, 512), F32),
            pltpu.VMEM((4, 24, 128), F32), pltpu.VMEM((3, most, 24, 128), F32),
            pltpu.VMEM((2, 64, 128), F32), pltpu.VMEM((2, 64, 128), F32),
            pltpu.VMEM((2, 16, 128), F32), pltpu.VMEM((2, 16, 128), F32),
            pltpu.VMEM((2, 5, 48, 128), F32),
            pltpu.VMEM((2, 64, 128), F32), pltpu.VMEM((2, 64, 128), F32),
            pltpu.VMEM((2, 16, 128), F32), pltpu.VMEM((2, 16, 128), F32),
            pltpu.VMEM((2, 3, 10, 8, 128), F32),
            dma((6,)), dma((6,)), dma((6,)), dma((6,)), dma((3, most)), dma((3, most)), dma((7,)),
        ],
        compiler_params=pltpu.CompilerParams(
            collective_id=0, has_side_effects=True, vmem_limit_bytes=40 * 1024 * 1024
        ),
        name="section",
    )(
        *(pltpu.with_memory_space_constraint(a, pltpu.HBM) for a in (
            density.reshape(64, 128), momentum.reshape(3, 64, 128), energy.reshape(64, 128),
            cotangent.reshape(5, 64, 128), w_in.T, b_in[None, :], w_out,
        ))
    )
    residual, adjoint, grad_w_in, grad_b_in, grad_w_out = pl.pallas_call(
        finish,
        out_shape=(
            block, block,
            jax.ShapeDtypeStruct((30, 64), F32), jax.ShapeDtypeStruct((1, 64), F32), jax.ShapeDtypeStruct((5, 64), F32),
        ),
        in_specs=[vmem] * 3,
        out_specs=(hbm,) * 5,
        scratch_shapes=[
            pltpu.VMEM((30, 64), F32), pltpu.VMEM((1, 64), F32), pltpu.VMEM((5, 64), F32), dma((5,)),
        ],
        compiler_params=pltpu.CompilerParams(vmem_limit_bytes=16 * 1024 * 1024),
        name="store",
    )(residual, adjoint, grads)
    return (
        residual.reshape(5, 4, 16, 128), adjoint.reshape(5, 4, 16, 128),
        grad_w_in.T, grad_b_in[0], grad_w_out,
    )


def solution(mesh):
    return jax.shard_map(
        per_device,
        mesh=mesh,
        in_specs=(
            P("gx", "gy", "gz"),
            P(None, "gx", "gy", "gz"),
            P("gx", "gy", "gz"),
            P(None, "gx", "gy", "gz"),
            P(),
            P(),
            P(),
        ),
        out_specs=(P(None, "gx", "gy", "gz"), P(None, "gx", "gy", "gz"), P(), P(), P()),
        check_vma=False,
    )
```

```python
import functools

import jax
import jax.numpy as jnp
from jax import lax
from jax.experimental import pallas as pl
from jax.experimental.pallas import tpu as pltpu
from jax.sharding import PartitionSpec as P

F32 = jnp.float32
BF16 = jnp.bfloat16
AXES = ("gx", "gy", "gz")
MESH = pl.DeviceIdType.MESH
EPSILON = 1e-06
XC = 14
NT = (((1,), (1,)), ((), ()))


def recip(value):
    guess = pl.reciprocal(value, approx=True)
    return guess * (2.0 - value * guess)


def dot(left, right):
    return jnp.dot(left, right, preferred_element_type=F32)


def dot_nt(left, right):
    return lax.dot_general(left, right, NT, preferred_element_type=F32)


def line_weno(cells, cots):
    faces = len(cots)
    total = len(cells)
    diff = [cells[i + 1] - cells[i] for i in range(total - 1)]
    second = [None] + [diff[i] - diff[i - 1] for i in range(1, total - 1)]
    half = [None] + [0.5 * s for s in second[1:]]
    square = [None] + [EPSILON + (13.0 / 12.0) * s * s for s in second[1:]]
    third = [None] + [second[i + 1] - second[i] for i in range(1, total - 2)]
    values = []
    d_cell = [None] * total
    d_diff = [None] * total
    d_half = [None] * total
    d_square = [None] * total
    d_third = [None] * total

    def add(store, index, value):
        store[index] = value if store[index] is None else store[index] + value

    for k in range(faces):
        d1, d2 = diff[k + 1], diff[k + 2]
        t1, t2 = third[k + 1], third[k + 2]
        twice = t1 + t1
        pa = d1 + half[k + 1]
        pb = 0.5 * (d1 + d2)
        pc = d2 - half[k + 3]
        ra = recip(square[k + 1] + pa * pa)
        rb = recip(square[k + 2] + pb * pb)
        rc = recip(square[k + 3] + pc * pc)
        wa = ra * ra
        wb = 6.0 * (rb * rb)
        wc = 3.0 * (rc * rc)
        norm = recip(wa + wb + wc)
        y = (wa * twice + wc * t2) * norm
        values.append(cells[k + 2] + (1.0 / 6.0) * (d1 + (d2 + d2) - y))
        g = cots[k]
        sixth = (1.0 / 6.0) * g
        gn = sixth * norm
        ga = gn * wa
        gb = gn * wb
        gc = gn * wc
        ta = ga * ra * (twice - y)
        tb = gb * rb * y
        tc = gc * rc * (t2 - y)
        qa = 4.0 * (pa * ta)
        qb = 2.0 * (pb * tb)
        qc = 4.0 * (pc * tc)
        add(d_cell, k + 2, g)
        add(d_diff, k + 1, sixth + qa - qb)
        add(d_diff, k + 2, (sixth + sixth) + qc - qb)
        add(d_half, k + 1, qa)
        add(d_half, k + 3, -qc)
        add(d_square, k + 1, ta)
        add(d_square, k + 2, -tb)
        add(d_square, k + 3, tc)
        add(d_third, k + 1, -(ga + ga))
        add(d_third, k + 2, -gc)
    for i in range(1, total - 1):
        value = (13.0 / 3.0) * second[i] * d_square[i]
        if d_half[i] is not None:
            value = value + 0.5 * d_half[i]
        if d_third[i - 1] is not None:
            value = value + d_third[i - 1]
        if d_third[i] is not None:
            value = value - d_third[i]
        add(d_diff, i, value)
        add(d_diff, i - 1, -value)
    for i in range(total - 1):
        add(d_cell, i + 1, d_diff[i])
        add(d_cell, i, -d_diff[i])
    return values, d_cell


def kernel(
    sizes, dens, mom, ener, cot, w_in_h, b_in_h, w_out_h,
    res_o, adj_o, grad_o,
    cotv, w_in, b_in, w_out, fea, dco, nat, lamn, vv, ll, fp, fm, dfp, dfm, dv, corr_s, res_s,
    zw, zl, w1, w1t, w2, w2t, hid, dpr, g1, g2, gm, ar, ar_in,
    ys, yr, zs, zr, xr, yb, ybr, zb, zbr, xbr,
    halo_send, halo_recv, back_send, back_recv, ar_send, ar_recv, load_sem, relay,
):
    me = [lax.axis_index(a) for a in AXES]

    def peer(axis, step):
        count = sizes[axis]
        return {AXES[axis]: lax.rem(me[axis] + (step % count), count)}

    bar = pltpu.get_barrier_semaphore()
    for axis in range(3):
        for step in (-1, 1):
            pl.semaphore_signal(bar, 1, device_id=peer(axis, step), device_id_type=MESH)

    def relay_send(turn):
        for axis in range(3):
            for side, step in enumerate((-1, 1)):
                pl.semaphore_signal(relay.at[turn, axis, side], 1, device_id=peer(axis, step), device_id_type=MESH)

    def relay_wait(turn):
        for axis in range(3):
            for side in range(2):
                pl.semaphore_wait(relay.at[turn, axis, side], 1)

    loads = [
        pltpu.make_async_copy(src, dst, load_sem.at[index])
        for index, (src, dst) in enumerate((
            (dens, nat.at[0]), (mom, nat.at[1:4]), (ener, nat.at[4]), (cot, cotv),
            (w_in_h, w_in), (b_in_h, b_in), (w_out_h, w_out),
        ))
    ]
    for copy in loads:
        copy.start()

    lane = lax.broadcasted_iota(jnp.int32, (64, 128), 1)
    low = lane < 64
    lane8 = lax.broadcasted_iota(jnp.int32, (3, 128), 1)
    low3 = lane8 < 64

    for copy in loads:
        copy.wait()
    lamn[...] = cotv[...].astype(F32)

    def swap(value):
        return pltpu.roll(value, 64, 1)

    fields = [(nat, zw, 3, v) for v in range(5)] + [(lamn, zl, 0, v) for v in range(5)]
    for first, second in zip(fields[0::2], fields[1::2]):
        both = jnp.concatenate([first[0][first[3]], second[0][second[3]]], axis=0)
        turned = jnp.transpose(both)
        upper, lower = turned[0:64], turned[64:128]
        first[1][first[3], first[2] : first[2] + 64, :] = jnp.where(low, upper, swap(lower))
        second[1][second[3], second[2] : second[2] + 64, :] = jnp.where(low, swap(upper), lower)
    for v in range(5):
        zs[0, 3 * v : 3 * v + 3, :] = zw[v, 3:6, :]
        zs[1, 3 * v : 3 * v + 3, :] = zw[v, 64:67, :]
        for j in range(3):
            at = (3 * v + j) * 4
            ys[0, at : at + 4, :] = nat[v, pl.ds(j, 4, stride=16), :]
            ys[1, at : at + 4, :] = nat[v, pl.ds(13 + j, 4, stride=16), :]

    pl.semaphore_wait(bar, 6)

    def remote(src, dst, send, recv, index, axis, step):
        return pltpu.make_async_remote_copy(
            src_ref=src, dst_ref=dst, send_sem=send.at[index], recv_sem=recv.at[index],
            device_id=peer(axis, step), device_id_type=MESH,
        )

    halo = [
        remote(nat.at[:, 0:48, :], xr.at[1], halo_send, halo_recv, 0, 0, -1),
        remote(nat.at[:, 16:64, :], xr.at[0], halo_send, halo_recv, 1, 0, 1),
        remote(ys.at[0], yr.at[1], halo_send, halo_recv, 2, 1, -1),
        remote(ys.at[1], yr.at[0], halo_send, halo_recv, 3, 1, 1),
        remote(zs.at[0], zr.at[1], halo_send, halo_recv, 4, 2, -1),
        remote(zs.at[1], zr.at[0], halo_send, halo_recv, 5, 2, 1),
    ]
    for copy in halo:
        copy.start()
    relay_send(0)

    def iota(shape, dim):
        return lax.broadcasted_iota(jnp.int32, shape, dim)

    def one_hot(shape, wide):
        return (iota(shape, wide) // 8 == iota(shape, 1 - wide)).astype(F32).astype(BF16)

    def same_row(shape):
        return (iota(shape, 0) % 8) == (iota(shape, 1) % 8)

    spread = one_hot((512, 64), 0)
    spread_t = one_hot((64, 512), 1)
    bias = b_in[...]
    bias_a = bias.astype(BF16).astype(F32)
    bias_b = (bias - bias_a).astype(BF16).astype(F32)
    bias_c = bias - bias_a - bias_b
    row = iota((256, 64), 0)
    bias_rows = jnp.where(row == 240, bias_a, jnp.where(row == 241, bias_b, jnp.where(row == 242, bias_c, 0.0)))
    tall_in = (dot(one_hot((256, 30), 0), w_in[...]) + bias_rows).astype(BF16)
    kept = same_row((512, 256)) | (iota((512, 256), 1) >= 240)
    w1[...] = jnp.where(kept, dot_nt(spread, tall_in), 0.0).astype(BF16)
    w1t[...] = jnp.where(same_row((240, 512)), dot(tall_in[0:240], spread_t), 0.0).astype(BF16)
    tall_out = dot(one_hot((48, 5), 0), w_out[...]).astype(BF16)
    w2[...] = jnp.where(same_row((48, 512)), dot(tall_out, spread_t), 0.0).astype(BF16)
    wide_out = dot_nt(spread, w_out[...]).astype(BF16)
    w2t[...] = jnp.where(same_row((512, 48)), dot(wide_out, one_hot((5, 48), 1)), 0.0).astype(BF16)

    for v in range(5):
        for i in range(4):
            for t in range(2):
                at = i * 16 + t * 8
                vv[XC + 3 + i, 5 * t + v] = nat[v, at : at + 8, :]
                ll[11 + i, 5 * t + v] = lamn[v, at : at + 8, :]
        for r in range(14):
            for h in range(2):
                y = 8 * h + r - 3
                if 0 <= y < 16:
                    vv[r, v, 4 * h : 4 * h + 4, :] = nat[v, pl.ds(y, 4, stride=16), :]
        for j in range(8):
            vv[3 + j, 5 + v] = zw[v, pl.ds(3 + j, 8, stride=8), :]
            ll[1 + j, 5 + v] = zl[v, pl.ds(j, 8, stride=8), :]
            for h in range(2):
                ll[1 + j, v, 4 * h : 4 * h + 4, :] = lamn[v, pl.ds(8 * h + j, 4, stride=16), :]
    for end in (0, 9, 10, 15):
        ll[end] = jnp.zeros((10, 8, 128), F32)
    dv[...] = jnp.zeros(dv.shape, F32)

    ones = jnp.ones((16, 256), BF16)
    blank = jnp.zeros((8, 256), F32)

    def tile_lanes(p):
        return pl.ds(256 * p if isinstance(p, int) else pl.multiple_of(256 * p, 256), 256)

    def network(p0, c0, l0, count, start=False):
        lane0 = 256 * p0 if isinstance(p0, int) else pl.multiple_of(256 * p0, 256)
        for f in range(count):
            cells = [vv[pl.ds(c0 + f, 6), 5 * t : 5 * t + 5].reshape(240, 128) for t in range(2)]
            feats = jnp.concatenate([jnp.concatenate(cells, axis=1).astype(BF16), ones], axis=0)
            steps = [
                (ll[l0 + f + 1, 5 * t : 5 * t + 5] - ll[l0 + f, 5 * t : 5 * t + 5]).reshape(40, 128) for t in range(2)
            ]
            dcorr = jnp.concatenate([jnp.concatenate(steps, axis=1), blank], axis=0).astype(BF16)
            lanes = tile_lanes(p0 + f)
            fea[:, lanes] = feats
            dco[:, lanes] = dcorr
            for part in range(4):
                rows = slice(128 * part, 128 * part + 128)
                act = jnp.tanh(dot(w1[rows, :], feats))
                hid[rows, lanes] = act.astype(BF16)
                dpr[rows, lanes] = (dot(w2t[rows, :], dcorr) * (1.0 - act * act)).astype(BF16)
        wide = pl.ds(lane0, 256 * count)
        part1 = dot_nt(fea[:, wide], dpr[:, wide])
        part2 = dot_nt(dco[:, wide], hid[:, wide])
        if start:
            g1[...] = part1
            g2[...] = part2
        else:
            g1[...] += part1
            g2[...] += part2

    def products(p0, c0, count):
        total = {}
        for f in range(count):
            lanes = tile_lanes(p0 + f)
            corr = dot(w2[...], hid[:, lanes])
            dfeat = dot(w1t[...], dpr[:, lanes])
            for t in range(2):
                tile = slice(128 * t, 128 * t + 128)
                corr_s[p0 + f, 5 * t : 5 * t + 5] = corr[0:40, tile].reshape(5, 8, 128)
                for c in range(6):
                    part = dfeat[40 * c : 40 * c + 40, tile].reshape(5, 8, 128)
                    total[f + c, t] = part if (f + c, t) not in total else total[f + c, t] + part
        for (c, t), part in total.items():
            dv[c0 + c, 5 * t : 5 * t + 5] += part

    network(3, 3, 3, 3, start=True)
    relay_wait(0)
    relay_send(1)

    for copy in halo[2:]:
        copy.wait_recv()
    for v in range(5):
        for j in range(3):
            at = (3 * v + j) * 4
            vv[j, v, 0:4, :] = yr[0, at : at + 4, :]
            vv[11 + j, v, 4:8, :] = yr[1, at : at + 4, :]
        zw[v, 0:3, :] = swap(jnp.where(low3, zw[v, 64:67, :], zr[0, 3 * v : 3 * v + 3, :]))
        zw[v, 67:70, :] = swap(jnp.where(low3, zr[1, 3 * v : 3 * v + 3, :], zw[v, 3:6, :]))
        for r in (0, 1, 2, 11, 12, 13):
            vv[r, 5 + v] = zw[v, pl.ds(r, 8, stride=8), :]

    def net_yz(i, carry):
        network(6 * i, 6 * i, 6 * i, 3)
        return carry

    lax.fori_loop(0, 2, net_yz, 0)
    relay_wait(1)
    relay_send(2)

    for copy in halo[:2]:
        copy.wait_recv()
    for v in range(5):
        for i in range(3):
            for t in range(2):
                at = i * 16 + t * 8
                vv[XC + i, 5 * t + v] = xr[0, v, at : at + 8, :]
                vv[XC + 7 + i, 5 * t + v] = xr[1, v, at : at + 8, :]
    network(9, XC, 10, 5)

    inner = jnp.where(same_row((240, 512)), g1[0:240, :], 0.0).reshape(30, 8, 512)
    outer = jnp.where(same_row((40, 512)), g2[0:40, :], 0.0).reshape(5, 8, 512)
    gm[0:30, :] = jnp.sum(inner, axis=1)
    gm[30:31, :] = g1[240:241, :]
    gm[31:36, :] = jnp.sum(outer, axis=1)
    gm[36:40, :] = jnp.zeros((4, 512), F32)
    gather = (iota((512, 128), 0) // 8 == iota((512, 128), 1)).astype(F32)
    packed = jnp.dot(gm[...], gather, preferred_element_type=F32, precision=lax.Precision.HIGHEST)
    gm[:, 0:128] = packed
    ar[0] = gm[0:18, 0:128] + swap(gm[18:36, 0:128])
    relay_wait(2)

    order = (2, 1, 0)

    def reduce_start(phase):
        axis = order[phase]
        copies = [
            pltpu.make_async_remote_copy(
                src_ref=ar.at[phase], dst_ref=ar_in.at[phase, me[axis]],
                send_sem=ar_send.at[phase, step], recv_sem=ar_recv.at[phase, step],
                device_id=peer(axis, step), device_id_type=MESH,
            )
            for step in range(1, sizes[axis])
        ]
        for copy in copies:
            copy.start()
        ar_in[phase, me[axis]] = ar[phase]
        return copies

    def reduce_end(phase, copies):
        for copy in copies:
            copy.wait_recv()
        total = ar_in[phase, 0]
        for rank in range(1, sizes[order[phase]]):
            total = total + ar_in[phase, rank]
        ar[phase + 1] = total

    def physics(cell, base, comp):
        u = [vv[cell, base + v] for v in range(5)]
        inverse = recip(u[0])
        speed = u[1 + comp] * inverse
        square = u[1] * u[1] + u[2] * u[2] + u[3] * u[3]
        pressure = 0.4 * (u[4] - 0.5 * square * inverse)
        return u, inverse, speed, square, pressure

    def split_flux(c0, count, base, comp):
        def step(c, carry):
            cell = c0 + c
            u, _, speed, _, pressure = physics(cell, base, comp)
            flux = [u[1 + comp]] + [u[1 + k] * speed for k in range(3)] + [(u[4] + pressure) * speed]
            flux[1 + comp] = flux[1 + comp] + pressure
            for v in range(5):
                part = 0.5 * flux[v]
                wave = 2.0 * u[v]
                fp[cell, base + v] = part + wave
                fm[cell, base + v] = part - wave
            return carry

        lax.fori_loop(0, count, step, 0, unroll=count // 2)

    def pull_flux(c0, count, base, comp):
        def step(c, carry):
            cell = c0 + c
            u, inverse, speed, square, pressure = physics(cell, base, comp)
            plus = [dfp[cell, base + v] for v in range(5)]
            minus = [dfm[cell, base + v] for v in range(5)]
            df = [0.5 * (a + b) for a, b in zip(plus, minus)]
            du = [2.0 * (a - b) for a, b in zip(plus, minus)]
            d_speed = df[4] * (u[4] + pressure)
            for k in range(3):
                d_speed = d_speed + df[1 + k] * u[1 + k]
            d_energy = df[4] * speed
            d_press = 0.4 * (df[1 + comp] + d_energy)
            slope = d_press * inverse
            du[4] = du[4] + d_energy + d_press
            for k in range(3):
                du[1 + k] = du[1 + k] + df[1 + k] * speed - slope * u[1 + k]
            du[1 + comp] = du[1 + comp] + df[0] + d_speed * inverse
            d_inverse = d_speed * u[1 + comp] - 0.5 * square * d_press
            du[0] = du[0] - inverse * inverse * d_inverse
            for v in range(5):
                dv[cell, base + v] += du[v]
            return carry

        lax.fori_loop(0, count, step, 0, unroll=count // 2)

    def weno(c0, l0, p0, r0, faces, first, last):
        def step(q, carry):
            plus = [fp[c0 + c, q] for c in range(faces + 4)]
            minus = [fm[c0 + c, q] for c in range(faces + 4, 0, -1)]
            lam = [ll[l0 + k, q] for k in range(faces + 1)]
            cots = [lam[k + 1] - lam[k] for k in range(faces)]
            value_p, d_plus = line_weno(plus, cots)
            value_m, d_minus = line_weno(minus, cots[::-1])
            flux = [value_p[k] + value_m[faces - 1 - k] + corr_s[p0 + k, q] for k in range(faces)]
            for c in range(faces - 1):
                res_s[r0 + c, q] = flux[c] - flux[c + 1]
            for c in range(faces + 4):
                dfp[c0 + c, q] = d_plus[c]
                dfm[c0 + faces + 4 - c, q] = d_minus[c]
            dfp[c0 + faces + 4, q] = jnp.zeros((8, 128), F32)
            dfm[c0, q] = jnp.zeros((8, 128), F32)
            return carry

        lax.fori_loop(first, last, step, 0)

    def back(src, dst, index, axis, step):
        return remote(src, dst, back_send, back_recv, index, axis, step)

    waiting = reduce_start(0)
    started = list(waiting)

    products(9, XC, 5)

    split_flux(XC, 10, 0, 0)
    split_flux(XC, 10, 5, 0)
    weno(XC, 10, 9, 8, 5, 0, 10)
    pull_flux(XC, 10, 0, 0)
    pull_flux(XC, 10, 5, 0)
    back_x = [back(dv.at[XC : XC + 3], xbr.at[1], 0, 0, -1), back(dv.at[XC + 7 : XC + 10], xbr.at[0], 1, 0, 1)]
    for copy in back_x:
        copy.start()

    def products_yz(i, carry):
        products(3 * i, 3 * i, 3)
        return carry

    lax.fori_loop(0, 3, products_yz, 0)

    reduce_end(0, waiting)
    waiting = reduce_start(1)
    started += waiting

    split_flux(0, 14, 5, 2)
    weno(0, 0, 0, 0, 9, 5, 10)
    pull_flux(0, 14, 5, 2)
    for v in range(5):
        for r in range(8):
            zw[v, pl.ds(r, 8, stride=8), :] = dv[r, 5 + v]
            zl[v, pl.ds(r, 8, stride=8), :] = res_s[r, 5 + v]
        zw[v, 64:72, :] = jnp.zeros((8, 128), F32)
        for r in range(8, 14):
            zw[v, pl.ds(r, 8, stride=8), :] += dv[r, 5 + v]
        zb[0, 3 * v : 3 * v + 3, :] = zw[v, 0:3, :]
        zb[1, 3 * v : 3 * v + 3, :] = zw[v, 67:70, :]
    back_z = [back(zb.at[0], zbr.at[1], 4, 2, -1), back(zb.at[1], zbr.at[0], 5, 2, 1)]
    for copy in back_z:
        copy.start()

    split_flux(0, 14, 0, 1)
    weno(0, 0, 0, 0, 9, 0, 5)
    pull_flux(0, 14, 0, 1)
    for v in range(5):
        for j in range(3):
            at = (3 * v + j) * 4
            yb[0, at : at + 4, :] = dv[j, v, 0:4, :]
            yb[1, at : at + 4, :] = dv[11 + j, v, 4:8, :]
    back_y = [back(yb.at[0], ybr.at[1], 2, 1, -1), back(yb.at[1], ybr.at[0], 3, 1, 1)]
    for copy in back_y:
        copy.start()

    for copy in back_z:
        copy.wait_recv()
    for v in range(5):
        near = zw[v, 0:3, :]
        far = zw[v, 67:70, :]
        zw[v, 64:67, :] += swap(jnp.where(low3, zbr[1, 3 * v : 3 * v + 3, :], near))
        zw[v, 3:6, :] += swap(jnp.where(low3, far, zbr[0, 3 * v : 3 * v + 3, :]))
    fields = [(zw, adj_o, 3, v) for v in range(5)] + [(zl, res_o, 0, v) for v in range(5)]
    for first, second in zip(fields[0::2], fields[1::2]):
        one = first[0][first[3], first[2] : first[2] + 64, :]
        two = second[0][second[3], second[2] : second[2] + 64, :]
        upper = jnp.where(low, one, swap(two))
        lower = jnp.where(low, swap(one), two)
        turned = jnp.transpose(jnp.concatenate([upper, lower], axis=0))
        first[1][first[3]] = turned[0:64]
        second[1][second[3]] = turned[64:128]

    reduce_end(1, waiting)
    waiting = reduce_start(2)
    started += waiting

    for copy in back_x:
        copy.wait_recv()
    for v in range(5):
        for i in range(4):
            for t in range(2):
                at = i * 16 + t * 8
                value = dv[XC + 3 + i, 5 * t + v]
                if i < 3:
                    value = value + xbr[0, i, 5 * t + v]
                if i > 0:
                    value = value + xbr[1, i - 1, 5 * t + v]
                adj_o[v, at : at + 8, :] += value
                res_o[v, at : at + 8, :] += res_s[8 + i, 5 * t + v]

    for v in range(5):
        for r in range(14):
            for h in range(2):
                y = 8 * h + r - 3
                if 0 <= y < 16:
                    adj_o[v, pl.ds(y, 4, stride=16), :] += dv[r, v, 4 * h : 4 * h + 4, :]
        for j in range(8):
            for h in range(2):
                res_o[v, pl.ds(8 * h + j, 4, stride=16), :] += res_s[j, v, 4 * h : 4 * h + 4, :]
    for copy in back_y:
        copy.wait_recv()
    for v in range(5):
        for j in range(3):
            at = (3 * v + j) * 4
            adj_o[v, pl.ds(j, 4, stride=16), :] += ybr[0, at : at + 4, :]
            adj_o[v, pl.ds(13 + j, 4, stride=16), :] += ybr[1, at : at + 4, :]

    reduce_end(2, waiting)
    grad_o[0:18, :] = ar[3]
    grad_o[18:36, :] = swap(ar[3])

    for copy in halo + started + back_x + back_y + back_z:
        copy.wait_send()


def finish(res, adj, grad, res_h, adj_h, gwi_h, gbi_h, gwo_h, gwi, gbi, gwo, sems):
    gwi[...] = grad[0:30, 0:64]
    gbi[...] = grad[30:31, 0:64]
    gwo[...] = grad[31:36, 0:64]
    pairs = ((res, res_h), (adj, adj_h), (gwi, gwi_h), (gbi, gbi_h), (gwo, gwo_h))
    copies = [pltpu.make_async_copy(src, dst, sems.at[index]) for index, (src, dst) in enumerate(pairs)]
    for copy in copies:
        copy.start()
    for copy in copies:
        copy.wait()


def per_device(density, momentum, energy, cotangent, w_in, b_in, w_out):
    sizes = tuple(lax.axis_size(a) for a in AXES)
    most = max(sizes)
    vmem = pl.BlockSpec(memory_space=pltpu.VMEM)
    hbm = pl.BlockSpec(memory_space=pltpu.HBM)
    tiles = lambda n: pltpu.VMEM((n, 10, 8, 128), F32)
    dma = pltpu.SemaphoreType.DMA
    block = jax.ShapeDtypeStruct((5, 64, 128), F32)
    residual, adjoint, grads = pl.pallas_call(
        functools.partial(kernel, sizes),
        out_shape=(block, block, jax.ShapeDtypeStruct((40, 128), F32)),
        in_specs=[hbm] * 7,
        out_specs=(vmem,) * 3,
        scratch_shapes=[
            pltpu.VMEM((5, 64, 128), BF16), pltpu.VMEM((30, 64), BF16),
            pltpu.VMEM((1, 64), F32), pltpu.VMEM((5, 64), BF16),
            pltpu.VMEM((256, 3584), BF16), pltpu.VMEM((48, 3584), BF16),
            pltpu.VMEM((5, 64, 128), F32), pltpu.VMEM((5, 64, 128), F32),
            tiles(24), tiles(16), tiles(24), tiles(24), tiles(24), tiles(24), tiles(24), tiles(14), tiles(12),
            pltpu.VMEM((5, 72, 128), F32), pltpu.VMEM((5, 64, 128), F32),
            pltpu.VMEM((512, 256), BF16), pltpu.VMEM((240, 512), BF16),
            pltpu.VMEM((48, 512), BF16), pltpu.VMEM((512, 48), BF16),
            pltpu.VMEM((512, 3584), BF16), pltpu.VMEM((512, 3584), BF16),
            pltpu.VMEM((256, 512), F32), pltpu.VMEM((48, 512), F32), pltpu.VMEM((40, 512), F32),
            pltpu.VMEM((4, 18, 128), F32), pltpu.VMEM((3, most, 18, 128), F32),
            pltpu.VMEM((2, 64, 128), F32), pltpu.VMEM((2, 64, 128), F32),
            pltpu.VMEM((2, 16, 128), F32), pltpu.VMEM((2, 16, 128), F32),
            pltpu.VMEM((2, 5, 48, 128), F32),
            pltpu.VMEM((2, 64, 128), F32), pltpu.VMEM((2, 64, 128), F32),
            pltpu.VMEM((2, 16, 128), F32), pltpu.VMEM((2, 16, 128), F32),
            pltpu.VMEM((2, 3, 10, 8, 128), F32),
            dma((6,)), dma((6,)), dma((6,)), dma((6,)), dma((3, most)), dma((3, most)), dma((7,)),
            pltpu.SemaphoreType.REGULAR((3, 3, 2)),
        ],
        compiler_params=pltpu.CompilerParams(
            collective_id=0, has_side_effects=True, vmem_limit_bytes=40 * 1024 * 1024
        ),
        name="section",
    )(
        *(pltpu.with_memory_space_constraint(a, pltpu.HBM) for a in (
            density.reshape(64, 128), momentum.reshape(3, 64, 128), energy.reshape(64, 128),
            cotangent.reshape(5, 64, 128), w_in.T, b_in[None, :], w_out,
        ))
    )
    residual, adjoint, grad_w_in, grad_b_in, grad_w_out = pl.pallas_call(
        finish,
        out_shape=(
            block, block,
            jax.ShapeDtypeStruct((30, 64), F32), jax.ShapeDtypeStruct((1, 64), F32), jax.ShapeDtypeStruct((5, 64), F32),
        ),
        in_specs=[vmem] * 3,
        out_specs=(hbm,) * 5,
        scratch_shapes=[
            pltpu.VMEM((30, 64), F32), pltpu.VMEM((1, 64), F32), pltpu.VMEM((5, 64), F32), dma((5,)),
        ],
        compiler_params=pltpu.CompilerParams(vmem_limit_bytes=16 * 1024 * 1024),
        name="store",
    )(residual, adjoint, grads)
    return (
        residual.reshape(5, 4, 16, 128), adjoint.reshape(5, 4, 16, 128),
        grad_w_in.T, grad_b_in[0], grad_w_out,
    )


def solution(mesh):
    return jax.shard_map(
        per_device,
        mesh=mesh,
        in_specs=(
            P("gx", "gy", "gz"),
            P(None, "gx", "gy", "gz"),
            P("gx", "gy", "gz"),
            P(None, "gx", "gy", "gz"),
            P(),
            P(),
            P(),
        ),
        out_specs=(P(None, "gx", "gy", "gz"), P(None, "gx", "gy", "gz"), P(), P(), P()),
        check_vma=False,
    )
```

```python
import functools

import jax
import jax.numpy as jnp
from jax import lax
from jax.experimental import pallas as pl
from jax.experimental.pallas import tpu as pltpu
from jax.sharding import PartitionSpec as P

F32 = jnp.float32
BF16 = jnp.bfloat16
AXES = ("gx", "gy", "gz")
MESH = pl.DeviceIdType.MESH
EPSILON = 1e-06
XC = 14
NT = (((1,), (1,)), ((), ()))


def recip(value):
    guess = pl.reciprocal(value, approx=True)
    return guess * (2.0 - value * guess)


def dot(left, right):
    return jnp.dot(left, right, preferred_element_type=F32)


def dot_nt(left, right):
    return lax.dot_general(left, right, NT, preferred_element_type=F32)


def line_weno(cells, cots):
    faces = len(cots)
    total = len(cells)
    diff = [cells[i + 1] - cells[i] for i in range(total - 1)]
    second = [None] + [diff[i] - diff[i - 1] for i in range(1, total - 1)]
    half = [None] + [0.5 * s for s in second[1:]]
    square = [None] + [EPSILON + (13.0 / 12.0) * s * s for s in second[1:]]
    third = [None] + [second[i + 1] - second[i] for i in range(1, total - 2)]
    values = []
    d_cell = [None] * total
    d_diff = [None] * total
    d_half = [None] * total
    d_square = [None] * total
    d_third = [None] * total

    def add(store, index, value):
        store[index] = value if store[index] is None else store[index] + value

    for k in range(faces):
        d1, d2 = diff[k + 1], diff[k + 2]
        t1, t2 = third[k + 1], third[k + 2]
        twice = t1 + t1
        pa = d1 + half[k + 1]
        pb = 0.5 * (d1 + d2)
        pc = d2 - half[k + 3]
        ra = recip(square[k + 1] + pa * pa)
        rb = recip(square[k + 2] + pb * pb)
        rc = recip(square[k + 3] + pc * pc)
        wa = ra * ra
        wb = 6.0 * (rb * rb)
        wc = 3.0 * (rc * rc)
        norm = recip(wa + wb + wc)
        y = (wa * twice + wc * t2) * norm
        values.append(cells[k + 2] + (1.0 / 6.0) * (d1 + (d2 + d2) - y))
        g = cots[k]
        sixth = (1.0 / 6.0) * g
        gn = sixth * norm
        ga = gn * wa
        gb = gn * wb
        gc = gn * wc
        ta = ga * ra * (twice - y)
        tb = gb * rb * y
        tc = gc * rc * (t2 - y)
        qa = 4.0 * (pa * ta)
        qb = 2.0 * (pb * tb)
        qc = 4.0 * (pc * tc)
        add(d_cell, k + 2, g)
        add(d_diff, k + 1, sixth + qa - qb)
        add(d_diff, k + 2, (sixth + sixth) + qc - qb)
        add(d_half, k + 1, qa)
        add(d_half, k + 3, -qc)
        add(d_square, k + 1, ta)
        add(d_square, k + 2, -tb)
        add(d_square, k + 3, tc)
        add(d_third, k + 1, -(ga + ga))
        add(d_third, k + 2, -gc)
    for i in range(1, total - 1):
        value = (13.0 / 3.0) * second[i] * d_square[i]
        if d_half[i] is not None:
            value = value + 0.5 * d_half[i]
        if d_third[i - 1] is not None:
            value = value + d_third[i - 1]
        if d_third[i] is not None:
            value = value - d_third[i]
        add(d_diff, i, value)
        add(d_diff, i - 1, -value)
    for i in range(total - 1):
        add(d_cell, i + 1, d_diff[i])
        add(d_cell, i, -d_diff[i])
    return values, d_cell


def kernel(
    sizes, dens, mom, ener, cot, w_in_h, b_in_h, w_out_h,
    res_o, adj_o, grad_o,
    cotv, w_in, b_in, w_out, fea, dco, nat, lamn, vv, ll, fp, fm, dfp, dfm, dv, corr_s, res_s,
    zw, zl, w1, w1t, w2, w2t, hid, dpr, g1, g2, gm, ar, ar_in,
    ys, yr, zs, zr, xr, yb, ybr, zb, zbr, xbr,
    halo_send, halo_recv, back_send, back_recv, ar_send, ar_recv, load_sem, relay,
):
    me = [lax.axis_index(a) for a in AXES]

    def peer(axis, step):
        count = sizes[axis]
        return {AXES[axis]: lax.rem(me[axis] + (step % count), count)}

    bar = pltpu.get_barrier_semaphore()
    for axis in range(3):
        for step in (-1, 1):
            pl.semaphore_signal(bar, 1, device_id=peer(axis, step), device_id_type=MESH)

    def relay_send(turn):
        for axis in range(3):
            for side, step in enumerate((-1, 1)):
                pl.semaphore_signal(relay.at[turn, axis, side], 1, device_id=peer(axis, step), device_id_type=MESH)

    def relay_wait(turn):
        for axis in range(3):
            for side in range(2):
                pl.semaphore_wait(relay.at[turn, axis, side], 1)

    loads = [
        pltpu.make_async_copy(src, dst, load_sem.at[index])
        for index, (src, dst) in enumerate((
            (dens, nat.at[0]), (mom, nat.at[1:4]), (ener, nat.at[4]), (cot, cotv),
            (w_in_h, w_in), (b_in_h, b_in), (w_out_h, w_out),
        ))
    ]
    for copy in loads:
        copy.start()

    lane = lax.broadcasted_iota(jnp.int32, (64, 128), 1)
    low = lane < 64
    lane8 = lax.broadcasted_iota(jnp.int32, (3, 128), 1)
    low3 = lane8 < 64

    for copy in loads:
        copy.wait()
    lamn[...] = cotv[...].astype(F32)

    def swap(value):
        return pltpu.roll(value, 64, 1)

    fields = [(nat, zw, 3, v) for v in range(5)] + [(lamn, zl, 0, v) for v in range(5)]
    for first, second in zip(fields[0::2], fields[1::2]):
        both = jnp.concatenate([first[0][first[3]], second[0][second[3]]], axis=0)
        turned = jnp.transpose(both)
        upper, lower = turned[0:64], turned[64:128]
        first[1][first[3], first[2] : first[2] + 64, :] = jnp.where(low, upper, swap(lower))
        second[1][second[3], second[2] : second[2] + 64, :] = jnp.where(low, swap(upper), lower)
    for v in range(5):
        zs[0, 3 * v : 3 * v + 3, :] = zw[v, 3:6, :]
        zs[1, 3 * v : 3 * v + 3, :] = zw[v, 64:67, :]
        for j in range(3):
            at = (3 * v + j) * 4
            ys[0, at : at + 4, :] = nat[v, pl.ds(j, 4, stride=16), :]
            ys[1, at : at + 4, :] = nat[v, pl.ds(13 + j, 4, stride=16), :]

    pl.semaphore_wait(bar, 6)

    def remote(src, dst, send, recv, index, axis, step):
        return pltpu.make_async_remote_copy(
            src_ref=src, dst_ref=dst, send_sem=send.at[index], recv_sem=recv.at[index],
            device_id=peer(axis, step), device_id_type=MESH,
        )

    halo = [
        remote(nat.at[:, 0:48, :], xr.at[1], halo_send, halo_recv, 0, 0, -1),
        remote(nat.at[:, 16:64, :], xr.at[0], halo_send, halo_recv, 1, 0, 1),
        remote(ys.at[0], yr.at[1], halo_send, halo_recv, 2, 1, -1),
        remote(ys.at[1], yr.at[0], halo_send, halo_recv, 3, 1, 1),
        remote(zs.at[0], zr.at[1], halo_send, halo_recv, 4, 2, -1),
        remote(zs.at[1], zr.at[0], halo_send, halo_recv, 5, 2, 1),
    ]
    for copy in halo:
        copy.start()
    relay_send(0)

    def iota(shape, dim):
        return lax.broadcasted_iota(jnp.int32, shape, dim)

    def one_hot(shape, wide):
        return (iota(shape, wide) // 8 == iota(shape, 1 - wide)).astype(F32).astype(BF16)

    def same_row(shape):
        return (iota(shape, 0) % 8) == (iota(shape, 1) % 8)

    spread = one_hot((512, 64), 0)
    spread_t = one_hot((64, 512), 1)
    bias = b_in[...]
    bias_a = bias.astype(BF16).astype(F32)
    bias_b = (bias - bias_a).astype(BF16).astype(F32)
    bias_c = bias - bias_a - bias_b
    row = iota((256, 64), 0)
    bias_rows = jnp.where(row == 240, bias_a, jnp.where(row == 241, bias_b, jnp.where(row == 242, bias_c, 0.0)))
    tall_in = (dot(one_hot((256, 30), 0), w_in[...]) + bias_rows).astype(BF16)
    kept = same_row((512, 256)) | (iota((512, 256), 1) >= 240)
    w1[...] = jnp.where(kept, dot_nt(spread, tall_in), 0.0).astype(BF16)
    w1t[...] = jnp.where(same_row((240, 512)), dot(tall_in[0:240], spread_t), 0.0).astype(BF16)
    tall_out = dot(one_hot((48, 5), 0), w_out[...]).astype(BF16)
    w2[...] = jnp.where(same_row((48, 512)), dot(tall_out, spread_t), 0.0).astype(BF16)
    wide_out = dot_nt(spread, w_out[...]).astype(BF16)
    w2t[...] = jnp.where(same_row((512, 48)), dot(wide_out, one_hot((5, 48), 1)), 0.0).astype(BF16)

    for v in range(5):
        for i in range(4):
            for t in range(2):
                at = i * 16 + t * 8
                vv[XC + 3 + i, 5 * t + v] = nat[v, at : at + 8, :]
                ll[11 + i, 5 * t + v] = lamn[v, at : at + 8, :]
        for r in range(14):
            for h in range(2):
                y = 8 * h + r - 3
                if 0 <= y < 16:
                    vv[r, v, 4 * h : 4 * h + 4, :] = nat[v, pl.ds(y, 4, stride=16), :]
        for j in range(8):
            vv[3 + j, 5 + v] = zw[v, pl.ds(3 + j, 8, stride=8), :]
            ll[1 + j, 5 + v] = zl[v, pl.ds(j, 8, stride=8), :]
            for h in range(2):
                ll[1 + j, v, 4 * h : 4 * h + 4, :] = lamn[v, pl.ds(8 * h + j, 4, stride=16), :]
    for end in (0, 9, 10, 15):
        ll[end] = jnp.zeros((10, 8, 128), F32)
    dv[...] = jnp.zeros(dv.shape, F32)

    ones = jnp.ones((16, 256), BF16)
    blank = jnp.zeros((8, 256), F32)

    def tile_lanes(p):
        return pl.ds(256 * p if isinstance(p, int) else pl.multiple_of(256 * p, 256), 256)

    def network(p0, c0, l0, count, start=False):
        lane0 = 256 * p0 if isinstance(p0, int) else pl.multiple_of(256 * p0, 256)
        for f in range(count):
            cells = [vv[pl.ds(c0 + f, 6), 5 * t : 5 * t + 5].reshape(240, 128) for t in range(2)]
            feats = jnp.concatenate([jnp.concatenate(cells, axis=1).astype(BF16), ones], axis=0)
            steps = [
                (ll[l0 + f + 1, 5 * t : 5 * t + 5] - ll[l0 + f, 5 * t : 5 * t + 5]).reshape(40, 128) for t in range(2)
            ]
            dcorr = jnp.concatenate([jnp.concatenate(steps, axis=1), blank], axis=0).astype(BF16)
            lanes = tile_lanes(p0 + f)
            fea[:, lanes] = feats
            dco[:, lanes] = dcorr
            for part in range(4):
                rows = slice(128 * part, 128 * part + 128)
                act = jnp.tanh(dot(w1[rows, :], feats))
                hid[rows, lanes] = act.astype(BF16)
                dpr[rows, lanes] = (dot(w2t[rows, :], dcorr) * (1.0 - act * act)).astype(BF16)
        wide = pl.ds(lane0, 256 * count)
        part1 = dot_nt(fea[:, wide], dpr[:, wide])
        part2 = dot_nt(dco[:, wide], hid[:, wide])
        if start:
            g1[...] = part1
            g2[...] = part2
        else:
            g1[...] += part1
            g2[...] += part2

    def products(p0, c0, count):
        total = {}
        for f in range(count):
            lanes = tile_lanes(p0 + f)
            corr = dot(w2[...], hid[:, lanes])
            dfeat = dot(w1t[...], dpr[:, lanes])
            for t in range(2):
                tile = slice(128 * t, 128 * t + 128)
                corr_s[p0 + f, 5 * t : 5 * t + 5] = corr[0:40, tile].reshape(5, 8, 128)
                for c in range(6):
                    part = dfeat[40 * c : 40 * c + 40, tile].reshape(5, 8, 128)
                    total[f + c, t] = part if (f + c, t) not in total else total[f + c, t] + part
        for (c, t), part in total.items():
            dv[c0 + c, 5 * t : 5 * t + 5] += part

    network(3, 3, 3, 3, start=True)
    relay_wait(0)
    relay_send(1)

    for copy in halo[2:]:
        copy.wait_recv()
    for v in range(5):
        for j in range(3):
            at = (3 * v + j) * 4
            vv[j, v, 0:4, :] = yr[0, at : at + 4, :]
            vv[11 + j, v, 4:8, :] = yr[1, at : at + 4, :]
        zw[v, 0:3, :] = swap(jnp.where(low3, zw[v, 64:67, :], zr[0, 3 * v : 3 * v + 3, :]))
        zw[v, 67:70, :] = swap(jnp.where(low3, zr[1, 3 * v : 3 * v + 3, :], zw[v, 3:6, :]))
        for r in (0, 1, 2, 11, 12, 13):
            vv[r, 5 + v] = zw[v, pl.ds(r, 8, stride=8), :]

    def net_yz(i, carry):
        network(6 * i, 6 * i, 6 * i, 3)
        return carry

    relay_wait(1)
    relay_send(2)
    lax.fori_loop(0, 2, net_yz, 0)

    for copy in halo[:2]:
        copy.wait_recv()
    for v in range(5):
        for i in range(3):
            for t in range(2):
                at = i * 16 + t * 8
                vv[XC + i, 5 * t + v] = xr[0, v, at : at + 8, :]
                vv[XC + 7 + i, 5 * t + v] = xr[1, v, at : at + 8, :]
    network(9, XC, 10, 5)

    inner = jnp.where(same_row((240, 512)), g1[0:240, :], 0.0).reshape(30, 8, 512)
    outer = jnp.where(same_row((40, 512)), g2[0:40, :], 0.0).reshape(5, 8, 512)
    gm[0:30, :] = jnp.sum(inner, axis=1)
    gm[30:31, :] = g1[240:241, :]
    gm[31:36, :] = jnp.sum(outer, axis=1)
    gm[36:40, :] = jnp.zeros((4, 512), F32)
    gather = (iota((512, 128), 0) // 8 == iota((512, 128), 1)).astype(F32)
    packed = jnp.dot(gm[...], gather, preferred_element_type=F32, precision=lax.Precision.HIGHEST)
    gm[:, 0:128] = packed
    ar[0] = gm[0:18, 0:128] + swap(gm[18:36, 0:128])
    relay_wait(2)

    order = (2, 1, 0)

    def reduce_start(phase):
        axis = order[phase]
        copies = [
            pltpu.make_async_remote_copy(
                src_ref=ar.at[phase], dst_ref=ar_in.at[phase, me[axis]],
                send_sem=ar_send.at[phase, step], recv_sem=ar_recv.at[phase, step],
                device_id=peer(axis, step), device_id_type=MESH,
            )
            for step in range(1, sizes[axis])
        ]
        for copy in copies:
            copy.start()
        ar_in[phase, me[axis]] = ar[phase]
        return copies

    def reduce_end(phase, copies):
        for copy in copies:
            copy.wait_recv()
        total = ar_in[phase, 0]
        for rank in range(1, sizes[order[phase]]):
            total = total + ar_in[phase, rank]
        ar[phase + 1] = total

    def physics(cell, base, comp):
        u = [vv[cell, base + v] for v in range(5)]
        inverse = recip(u[0])
        speed = u[1 + comp] * inverse
        square = u[1] * u[1] + u[2] * u[2] + u[3] * u[3]
        pressure = 0.4 * (u[4] - 0.5 * square * inverse)
        return u, inverse, speed, square, pressure

    def split_flux(c0, count, base, comp):
        def step(c, carry):
            cell = c0 + c
            u, _, speed, _, pressure = physics(cell, base, comp)
            flux = [u[1 + comp]] + [u[1 + k] * speed for k in range(3)] + [(u[4] + pressure) * speed]
            flux[1 + comp] = flux[1 + comp] + pressure
            for v in range(5):
                part = 0.5 * flux[v]
                wave = 2.0 * u[v]
                fp[cell, base + v] = part + wave
                fm[cell, base + v] = part - wave
            return carry

        lax.fori_loop(0, count, step, 0, unroll=count // 2)

    def pull_flux(c0, count, base, comp):
        def step(c, carry):
            cell = c0 + c
            u, inverse, speed, square, pressure = physics(cell, base, comp)
            plus = [dfp[cell, base + v] for v in range(5)]
            minus = [dfm[cell, base + v] for v in range(5)]
            df = [0.5 * (a + b) for a, b in zip(plus, minus)]
            du = [2.0 * (a - b) for a, b in zip(plus, minus)]
            d_speed = df[4] * (u[4] + pressure)
            for k in range(3):
                d_speed = d_speed + df[1 + k] * u[1 + k]
            d_energy = df[4] * speed
            d_press = 0.4 * (df[1 + comp] + d_energy)
            slope = d_press * inverse
            du[4] = du[4] + d_energy + d_press
            for k in range(3):
                du[1 + k] = du[1 + k] + df[1 + k] * speed - slope * u[1 + k]
            du[1 + comp] = du[1 + comp] + df[0] + d_speed * inverse
            d_inverse = d_speed * u[1 + comp] - 0.5 * square * d_press
            du[0] = du[0] - inverse * inverse * d_inverse
            for v in range(5):
                dv[cell, base + v] += du[v]
            return carry

        lax.fori_loop(0, count, step, 0, unroll=count // 2)

    def weno(c0, l0, p0, r0, faces, first, last):
        def step(q, carry):
            plus = [fp[c0 + c, q] for c in range(faces + 4)]
            minus = [fm[c0 + c, q] for c in range(faces + 4, 0, -1)]
            lam = [ll[l0 + k, q] for k in range(faces + 1)]
            cots = [lam[k + 1] - lam[k] for k in range(faces)]
            value_p, d_plus = line_weno(plus, cots)
            value_m, d_minus = line_weno(minus, cots[::-1])
            flux = [value_p[k] + value_m[faces - 1 - k] + corr_s[p0 + k, q] for k in range(faces)]
            for c in range(faces - 1):
                res_s[r0 + c, q] = flux[c] - flux[c + 1]
            for c in range(faces + 4):
                dfp[c0 + c, q] = d_plus[c]
                dfm[c0 + faces + 4 - c, q] = d_minus[c]
            dfp[c0 + faces + 4, q] = jnp.zeros((8, 128), F32)
            dfm[c0, q] = jnp.zeros((8, 128), F32)
            return carry

        lax.fori_loop(first, last, step, 0)

    def back(src, dst, index, axis, step):
        return remote(src, dst, back_send, back_recv, index, axis, step)

    waiting = reduce_start(0)
    started = list(waiting)

    products(9, XC, 5)

    split_flux(XC, 10, 0, 0)
    split_flux(XC, 10, 5, 0)
    weno(XC, 10, 9, 8, 5, 0, 10)
    pull_flux(XC, 10, 0, 0)
    pull_flux(XC, 10, 5, 0)
    back_x = [back(dv.at[XC : XC + 3], xbr.at[1], 0, 0, -1), back(dv.at[XC + 7 : XC + 10], xbr.at[0], 1, 0, 1)]
    for copy in back_x:
        copy.start()

    def products_yz(i, carry):
        products(3 * i, 3 * i, 3)
        return carry

    lax.fori_loop(0, 3, products_yz, 0)

    reduce_end(0, waiting)
    waiting = reduce_start(1)
    started += waiting

    split_flux(0, 14, 5, 2)
    weno(0, 0, 0, 0, 9, 5, 10)
    pull_flux(0, 14, 5, 2)
    for v in range(5):
        for r in range(8):
            zw[v, pl.ds(r, 8, stride=8), :] = dv[r, 5 + v]
            zl[v, pl.ds(r, 8, stride=8), :] = res_s[r, 5 + v]
        zw[v, 64:72, :] = jnp.zeros((8, 128), F32)
        for r in range(8, 14):
            zw[v, pl.ds(r, 8, stride=8), :] += dv[r, 5 + v]
        zb[0, 3 * v : 3 * v + 3, :] = zw[v, 0:3, :]
        zb[1, 3 * v : 3 * v + 3, :] = zw[v, 67:70, :]
    back_z = [back(zb.at[0], zbr.at[1], 4, 2, -1), back(zb.at[1], zbr.at[0], 5, 2, 1)]
    for copy in back_z:
        copy.start()

    split_flux(0, 14, 0, 1)
    weno(0, 0, 0, 0, 9, 0, 5)
    pull_flux(0, 14, 0, 1)
    for v in range(5):
        for j in range(3):
            at = (3 * v + j) * 4
            yb[0, at : at + 4, :] = dv[j, v, 0:4, :]
            yb[1, at : at + 4, :] = dv[11 + j, v, 4:8, :]
    back_y = [back(yb.at[0], ybr.at[1], 2, 1, -1), back(yb.at[1], ybr.at[0], 3, 1, 1)]
    for copy in back_y:
        copy.start()

    for copy in back_z:
        copy.wait_recv()
    for v in range(5):
        near = zw[v, 0:3, :]
        far = zw[v, 67:70, :]
        zw[v, 64:67, :] += swap(jnp.where(low3, zbr[1, 3 * v : 3 * v + 3, :], near))
        zw[v, 3:6, :] += swap(jnp.where(low3, far, zbr[0, 3 * v : 3 * v + 3, :]))
    fields = [(zw, adj_o, 3, v) for v in range(5)] + [(zl, res_o, 0, v) for v in range(5)]
    for first, second in zip(fields[0::2], fields[1::2]):
        one = first[0][first[3], first[2] : first[2] + 64, :]
        two = second[0][second[3], second[2] : second[2] + 64, :]
        upper = jnp.where(low, one, swap(two))
        lower = jnp.where(low, swap(one), two)
        turned = jnp.transpose(jnp.concatenate([upper, lower], axis=0))
        first[1][first[3]] = turned[0:64]
        second[1][second[3]] = turned[64:128]

    reduce_end(1, waiting)
    waiting = reduce_start(2)
    started += waiting

    for copy in back_x:
        copy.wait_recv()
    for v in range(5):
        for i in range(4):
            for t in range(2):
                at = i * 16 + t * 8
                value = dv[XC + 3 + i, 5 * t + v]
                if i < 3:
                    value = value + xbr[0, i, 5 * t + v]
                if i > 0:
                    value = value + xbr[1, i - 1, 5 * t + v]
                adj_o[v, at : at + 8, :] += value
                res_o[v, at : at + 8, :] += res_s[8 + i, 5 * t + v]

    for v in range(5):
        for r in range(14):
            for h in range(2):
                y = 8 * h + r - 3
                if 0 <= y < 16:
                    adj_o[v, pl.ds(y, 4, stride=16), :] += dv[r, v, 4 * h : 4 * h + 4, :]
        for j in range(8):
            for h in range(2):
                res_o[v, pl.ds(8 * h + j, 4, stride=16), :] += res_s[j, v, 4 * h : 4 * h + 4, :]
    for copy in back_y:
        copy.wait_recv()
    for v in range(5):
        for j in range(3):
            at = (3 * v + j) * 4
            adj_o[v, pl.ds(j, 4, stride=16), :] += ybr[0, at : at + 4, :]
            adj_o[v, pl.ds(13 + j, 4, stride=16), :] += ybr[1, at : at + 4, :]

    reduce_end(2, waiting)
    grad_o[0:18, :] = ar[3]
    grad_o[18:36, :] = swap(ar[3])

    for copy in halo + started + back_x + back_y + back_z:
        copy.wait_send()


def finish(res, adj, grad, res_h, adj_h, gwi_h, gbi_h, gwo_h, gwi, gbi, gwo, sems):
    gwi[...] = grad[0:30, 0:64]
    gbi[...] = grad[30:31, 0:64]
    gwo[...] = grad[31:36, 0:64]
    pairs = ((res, res_h), (adj, adj_h), (gwi, gwi_h), (gbi, gbi_h), (gwo, gwo_h))
    copies = [pltpu.make_async_copy(src, dst, sems.at[index]) for index, (src, dst) in enumerate(pairs)]
    for copy in copies:
        copy.start()
    for copy in copies:
        copy.wait()


def per_device(density, momentum, energy, cotangent, w_in, b_in, w_out):
    sizes = tuple(lax.axis_size(a) for a in AXES)
    most = max(sizes)
    vmem = pl.BlockSpec(memory_space=pltpu.VMEM)
    hbm = pl.BlockSpec(memory_space=pltpu.HBM)
    tiles = lambda n: pltpu.VMEM((n, 10, 8, 128), F32)
    dma = pltpu.SemaphoreType.DMA
    block = jax.ShapeDtypeStruct((5, 64, 128), F32)
    residual, adjoint, grads = pl.pallas_call(
        functools.partial(kernel, sizes),
        out_shape=(block, block, jax.ShapeDtypeStruct((40, 128), F32)),
        in_specs=[hbm] * 7,
        out_specs=(vmem,) * 3,
        scratch_shapes=[
            pltpu.VMEM((5, 64, 128), BF16), pltpu.VMEM((30, 64), BF16),
            pltpu.VMEM((1, 64), F32), pltpu.VMEM((5, 64), BF16),
            pltpu.VMEM((256, 3584), BF16), pltpu.VMEM((48, 3584), BF16),
            pltpu.VMEM((5, 64, 128), F32), pltpu.VMEM((5, 64, 128), F32),
            tiles(24), tiles(16), tiles(24), tiles(24), tiles(24), tiles(24), tiles(24), tiles(14), tiles(12),
            pltpu.VMEM((5, 72, 128), F32), pltpu.VMEM((5, 64, 128), F32),
            pltpu.VMEM((512, 256), BF16), pltpu.VMEM((240, 512), BF16),
            pltpu.VMEM((48, 512), BF16), pltpu.VMEM((512, 48), BF16),
            pltpu.VMEM((512, 3584), BF16), pltpu.VMEM((512, 3584), BF16),
            pltpu.VMEM((256, 512), F32), pltpu.VMEM((48, 512), F32), pltpu.VMEM((40, 512), F32),
            pltpu.VMEM((4, 18, 128), F32), pltpu.VMEM((3, most, 18, 128), F32),
            pltpu.VMEM((2, 64, 128), F32), pltpu.VMEM((2, 64, 128), F32),
            pltpu.VMEM((2, 16, 128), F32), pltpu.VMEM((2, 16, 128), F32),
            pltpu.VMEM((2, 5, 48, 128), F32),
            pltpu.VMEM((2, 64, 128), F32), pltpu.VMEM((2, 64, 128), F32),
            pltpu.VMEM((2, 16, 128), F32), pltpu.VMEM((2, 16, 128), F32),
            pltpu.VMEM((2, 3, 10, 8, 128), F32),
            dma((6,)), dma((6,)), dma((6,)), dma((6,)), dma((3, most)), dma((3, most)), dma((7,)),
            pltpu.SemaphoreType.REGULAR((3, 3, 2)),
        ],
        compiler_params=pltpu.CompilerParams(
            collective_id=0, has_side_effects=True, vmem_limit_bytes=40 * 1024 * 1024
        ),
        name="section",
    )(
        *(pltpu.with_memory_space_constraint(a, pltpu.HBM) for a in (
            density.reshape(64, 128), momentum.reshape(3, 64, 128), energy.reshape(64, 128),
            cotangent.reshape(5, 64, 128), w_in.T, b_in[None, :], w_out,
        ))
    )
    residual, adjoint, grad_w_in, grad_b_in, grad_w_out = pl.pallas_call(
        finish,
        out_shape=(
            block, block,
            jax.ShapeDtypeStruct((30, 64), F32), jax.ShapeDtypeStruct((1, 64), F32), jax.ShapeDtypeStruct((5, 64), F32),
        ),
        in_specs=[vmem] * 3,
        out_specs=(hbm,) * 5,
        scratch_shapes=[
            pltpu.VMEM((30, 64), F32), pltpu.VMEM((1, 64), F32), pltpu.VMEM((5, 64), F32), dma((5,)),
        ],
        compiler_params=pltpu.CompilerParams(vmem_limit_bytes=16 * 1024 * 1024),
        name="store",
    )(residual, adjoint, grads)
    return (
        residual.reshape(5, 4, 16, 128), adjoint.reshape(5, 4, 16, 128),
        grad_w_in.T, grad_b_in[0], grad_w_out,
    )


def solution(mesh):
    return jax.shard_map(
        per_device,
        mesh=mesh,
        in_specs=(
            P("gx", "gy", "gz"),
            P(None, "gx", "gy", "gz"),
            P("gx", "gy", "gz"),
            P(None, "gx", "gy", "gz"),
            P(),
            P(),
            P(),
        ),
        out_specs=(P(None, "gx", "gy", "gz"), P(None, "gx", "gy", "gz"), P(), P(), P()),
        check_vma=False,
    )
```
